32 devices in a mesh: lag: 16 (over z, x, core), pts: 2 (over y).
Axes of the slice: x: 2, y: 2, z: 4, core: 2. Of those that a mesh axis runs over, the one named last changes fastest.
Arguments:
- history: bfloat16 [96, 512, 128], P('lag'), may hold values from -6 to 6
- incident: bfloat16 [4, 512, 128], P(None, 'pts'), may hold values from -6 to 6
- kernel_blocks: bfloat16 [6144, 128, 128], P(('lag', 'pts')), may hold values from -0.013671875 to 0.013671875
- block_row: int32 [6144], P(('lag', 'pts')), may hold values from 0 to 1
- block_col: int32 [6144], P(('lag', 'pts')), may hold values from 0 to 3
- lag_offset: int32 [6144], P(('lag', 'pts')), may hold values from 0 to 5
- mode_kernel: float32 [96, 128], P('lag'), may hold values from 0.25 to 2
- self_inverse: float32 [512, 128], P('pts'), as said below
Outputs:
- densities: float32 [4, 512, 128], P(None, 'pts')
The draws below stay inside these ranges and needn't reach their ends.
Inputs may be any that keep to these rules, and one draw needn't show every extreme that they name: Each point block of self_inverse is the identity plus independent entries.
All inputs are finite; a program needn't handle non-finite values.
Results may differ from the reference program's by a relative error of at most 0.00031.
Values may be sent and summed in bfloat16 or wider, within the bound.
A program may use at most 128 MiB of HBM per device.

```python
import math
import jax
import jax.numpy as jnp
from jax import lax

MC = 128
B = 128
LAG_DEV = 6
NBLK = 192
STEPS = 4
PT_GROUPS = 2
NP = 512
LAGS = 96
ROWB = 2
NCB = 4
BLOCKS = 6144


def pinned_draw(key, salt, upper):
    position = jnp.arange(BLOCKS, dtype=jnp.int32) % NBLK
    values = jax.random.randint(jax.random.fold_in(key, salt), (BLOCKS,), 0, upper, dtype=jnp.int32)
    values = jnp.where(position == 0, 0, jnp.where(position == 1, upper - 1, values))
    return values.astype(jnp.int32)


def draw_block_row(key, part):
    return pinned_draw(key, 11, ROWB)


def draw_block_col(key, part):
    return pinned_draw(key, 23, NCB)


def draw_lag_offset(key, part):
    return pinned_draw(key, 37, LAG_DEV)


def draw_self_inverse(key, part):
    identity = (jnp.arange(NP)[:, None] % B == jnp.arange(B)[None, :]).astype(jnp.float32)
    noise = 0.35 * jax.random.normal(jax.random.fold_in(key, 5), (NP, B), jnp.float32)
    return (identity + noise / jnp.sqrt(jnp.float32(B))).astype(jnp.float32)


def shard_levels(key, shape, pieces, low, top_value):
    level, own = 1.0, jax.random.fold_in(key, 6)
    for dim, blocks in pieces:
        heights = jnp.exp(jax.random.uniform(jax.random.fold_in(own, dim), (blocks,), jnp.float32, low / len(pieces), top_value / len(pieces)))
        level = level * jnp.repeat(heights, shape[dim] // blocks).reshape([-1 if axis == dim else 1 for axis in range(len(shape))])
    return level


def bell_draw(stream_key, dims, width, most, cuts=(), kind=jnp.bfloat16):
    values = jax.random.normal(stream_key, dims, jnp.float32) * width
    if len(cuts) > 0:
        values = shard_levels(stream_key, dims, cuts, -0.22, 0.18) * values
    return jnp.clip(values, min=-most, max=most).astype(kind)


def setup_inputs(seed: int = 0) -> dict:
    key_of = jax.random.split(jax.random.key(seed), 9)
    history = bell_draw(key_of[0], (LAGS, NP, MC), 1.0, 6.0, ((0, 16),))
    incident = bell_draw(key_of[1], (STEPS, NP, MC), 1.0, 6.0, ((1, 2),))
    kernel_blocks = bell_draw(key_of[2], (BLOCKS, B, B), (B * NBLK * LAGS // (ROWB * LAG_DEV)) ** -0.5, 0.013671875, ((0, 32),))
    block_row = draw_block_row(jax.random.fold_in(key_of[8], 71), 0)
    block_col = draw_block_col(jax.random.fold_in(key_of[8], 71), 0)
    lag_offset = draw_lag_offset(jax.random.fold_in(key_of[8], 71), 0)
    mode_kernel = jnp.clip(jnp.exp(math.log(2.0) - 2.0794415 * jax.random.uniform(key_of[6], (LAGS, MC), jnp.float32) ** shard_levels(key_of[6], (LAGS, MC), ((0, 16),), -0.2, 0.2)), 0.25, 2.0)
    self_inverse = draw_self_inverse(jax.random.fold_in(key_of[8], 71), 0)
    return dict(history=history, incident=incident, kernel_blocks=kernel_blocks, block_row=block_row, block_col=block_col, lag_offset=lag_offset, mode_kernel=mode_kernel, self_inverse=self_inverse)


def reference(history, incident, kernel_blocks, block_row, block_col, lag_offset, mode_kernel, self_inverse):
    owner_group = jnp.arange(BLOCKS, dtype=jnp.int32) // NBLK
    global_row = ((owner_group % PT_GROUPS) * ROWB + block_row).astype(jnp.int32)
    global_lag = ((owner_group // PT_GROUPS) * LAG_DEV + lag_offset).astype(jnp.int32)
    inverse_blocks = self_inverse.reshape(NCB, B, B)
    state = history
    outputs = []
    for instant in range(STEPS):
        by_block = state.reshape(LAGS, NCB, B, MC)

        def add_group(lag_total, group_index):
            first_row = (group_index * NBLK).astype(jnp.int32)
            rows_of = lax.dynamic_slice_in_dim(global_row, first_row, NBLK)
            lags_of = lax.dynamic_slice_in_dim(global_lag, first_row, NBLK)
            cols_of = lax.dynamic_slice_in_dim(block_col, first_row, NBLK)
            kernels = lax.dynamic_slice_in_dim(kernel_blocks, first_row, NBLK).astype(jnp.float32)
            picked = by_block[lags_of, cols_of].astype(jnp.float32)
            products = jnp.einsum("eij,ejm->eim", kernels, picked, precision=lax.Precision.HIGHEST)
            products = products * mode_kernel[lags_of][:, None, :]
            return lag_total.at[rows_of].add(products), None

        start_total = jnp.zeros((NCB, B, MC), jnp.float32)
        lag_total, unused = lax.scan(add_group, start_total, jnp.arange(BLOCKS // NBLK, dtype=jnp.int32))
        net_field = incident[instant].astype(jnp.float32).reshape(NCB, B, MC) - lag_total
        density = jnp.einsum("cij,cjm->cim", inverse_blocks, net_field, precision=lax.Precision.HIGHEST).reshape(NP, MC)
        outputs.append(density)
        state = jnp.concatenate([density.astype(jnp.bfloat16)[None], state[:-1]], axis=0)
    return jnp.stack(outputs)
```

```python
import functools
import jax
import jax.numpy as jnp
from jax import lax
from jax.experimental import pallas as pl
from jax.experimental.pallas import tpu as pltpu
from jax.sharding import PartitionSpec as P

STEPS = 4
BACK = STEPS - 1
MESH = pl.DeviceIdType.MESH
HIGHEST = lax.Precision.HIGHEST
VMEM_BYTES = 48 * 1024 * 1024


def split_dot(pair, x):
    both = jnp.dot(pair, x, preferred_element_type=jnp.float32)
    half = both.shape[0] // 2
    return both[:half] + both[half:]


def split_rows(value):
    head = value.astype(jnp.bfloat16)
    rest = (value - head.astype(jnp.float32)).astype(jnp.bfloat16)
    return head, rest


def history_kernel(
    chunk, row_ref, col_ref, lag_ref, k_ref, hist_ref, mk_ref, part_ref, pair_ref, even, odd, work
):
    step = pl.program_id(0)
    lags, rows, points = even.shape
    size = k_ref.shape[1]
    modes = hist_ref.shape[2]

    @pl.when(step == 0)
    def _():
        even[...] = jnp.zeros_like(even)
        odd[...] = jnp.zeros_like(odd)

    def add(total, i):
        e = step * chunk + i
        r = pl.multiple_of(row_ref[e] * size, size)
        c = pl.multiple_of(col_ref[e] * size, size)
        total[lag_ref[e], pl.ds(r, size), pl.ds(c, size)] += k_ref[i].astype(jnp.float32)

    def body(j, carry):
        add(even, 2 * j)
        add(odd, 2 * j + 1)
        return carry

    lax.fori_loop(0, chunk // 2, body, 0, unroll=2)

    @pl.when(step == pl.num_programs(0) - 1)
    def _():
        for l in range(lags):
            head, rest = split_rows(even[l] + odd[l])
            target = pair_ref.at[l] if l < BACK else work
            target[:rows, :] = head
            target[rows:, :] = rest
            count = min(l, BACK) + 1
            x = jnp.concatenate([hist_ref[l - s] for s in range(count)], axis=1)
            found = split_dot(target[...], x)
            for s in range(STEPS):
                if s < count:
                    term = found[:, s * modes:(s + 1) * modes] * mk_ref[l:l + 1, :]
                    if l == s:
                        part_ref[s] = term
                    else:
                        part_ref[s] += term


def march_kernel(
    n, group, groups, n_pts,
    part_ref, pair_ref, halo_ref, mk_ref, inc_ref, inv_ref, out_ref,
    field, got1, sum1, got2, sum2, root_field, solved_pair, slabs, full,
    s1, r1, s2, r2, s3, r3, s4, r4, s5, r5, s6, r6, sx, rx,
):
    me = lax.axis_index("lag")
    mine = lax.axis_index("pts")
    g = lax.rem(me, group)
    z = me // group
    rows = part_ref.shape[1]
    modes = part_ref.shape[2]
    points = halo_ref.shape[1]
    size = inv_ref.shape[1]
    row_blocks = rows // size
    wide = rows // group
    thin = rows // n
    is_root = me == 0

    barrier = pltpu.get_barrier_semaphore()

    def greet(k, carry):
        pl.semaphore_signal(
            barrier, inc=1, device_id={"lag": lax.rem(me + k, n)}, device_id_type=MESH
        )
        return carry

    lax.fori_loop(1, n, greet, 0)

    for k in range(1, n_pts):
        pl.semaphore_signal(
            barrier, inc=1, device_id={"pts": lax.rem(mine + k, n_pts)}, device_id_type=MESH
        )

    def to(device, src, dst, send, recv):
        return pltpu.make_async_remote_copy(
            src_ref=src, dst_ref=dst, send_sem=send, recv_sem=recv,
            device_id=device, device_id_type=MESH,
        )

    def in_group(k):
        return lax.rem(g + k, group)

    def in_column(k):
        return lax.rem(z + k, groups)

    def span(first, count):
        return pl.ds(pl.multiple_of(first * count, count), count)

    other = {"lag": lax.rem(me + 1, n)}

    def copies1(s):
        for k in range(1, group):
            peer = in_group(k)
            yield to({"lag": z * group + peer}, field.at[s, span(peer, wide)],
                     got1.at[s, k - 1], s1.at[s, k - 1], r1.at[s])

    def copies2(s):
        for k in range(1, groups):
            peer = in_column(k)
            yield to({"lag": peer * group + g}, sum1.at[s, span(peer, thin)],
                     got2.at[s, k - 1], s2.at[s, k - 1], r2.at[s])

    share = span(g * groups + z, thin)

    def copy3(s):
        return to({"lag": 0}, sum2.at[s], root_field.at[s, share], s3.at[s], r3.at[s])

    def local_part(s):
        total = part_ref[s]
        for l in range(s):
            total += mk_ref[l:l + 1, :] * split_dot(pair_ref[l], halo_ref[BACK + l - s])
        field[s] = total

    def reduce1(s):
        for copy in copies1(s):
            copy.start()

    def reduce2(s):
        to(other, got1.at[s], got1.at[s], s1.at[s, 0], r1.at[s]).wait_recv()
        total = field[s, span(g, wide), :]
        for k in range(group - 1):
            total += got1[s, k]
        sum1[s] = total
        for copy in copies2(s):
            copy.start()

    def reduce3(s):
        to(other, got2.at[s], got2.at[s], s2.at[s, 0], r2.at[s]).wait_recv()
        total = sum1[s, span(z, thin), :]
        for k in range(groups - 1):
            total += got2[s, k]

        @pl.when(is_root)
        def _():
            root_field[s, 0:thin, :] = total

        @pl.when(jnp.logical_not(is_root))
        def _():
            sum2[s] = total
            copy3(s).start()

    def solve(value, r):
        return jnp.dot(inv_ref[r * size:(r + 1) * size, :], value,
                       precision=HIGHEST, preferred_element_type=jnp.float32)

    def solve_pairs():
        for l in range(BACK):
            for r in range(row_blocks):
                block = slice(r * size, (r + 1) * size)
                below = slice(rows + r * size, rows + (r + 1) * size)
                value = (pair_ref[l, block, :].astype(jnp.float32)
                         + pair_ref[l, below, :].astype(jnp.float32))
                head, rest = split_rows(solve(value, r))
                solved_pair[l, block, :] = head
                solved_pair[l, below, :] = rest

    def copies_x(s):
        for k in range(1, n_pts):
            here = slabs.at[s, span(mine, rows)]
            yield to({"pts": lax.rem(mine + k, n_pts)}, here, here, sx.at[s, k - 1], rx.at[s])

    def copy4(s, j):
        part = span(lax.rem(j, group) * groups + j // group, thin)
        return to({"lag": j}, full.at[s, part], full.at[s, part], s4.at[s], r4.at[s])

    def copies5(s):
        for k in range(1, groups):
            peer = in_column(k) * group + g
            here = full.at[s, share]
            yield peer, to({"lag": peer}, here, here, s5.at[s, k - 1], r5.at[s])

    def copies6(s):
        for k in range(1, group):
            peer = z * group + in_group(k)
            here = full.at[s, span(g, wide)]
            yield peer, to({"lag": peer}, here, here, s6.at[s, k - 1], r6.at[s])

    def march(s):
        rest = root_field.at[s, pl.ds(thin, rows - thin)]
        to(other, rest, rest, s3.at[s], r3.at[s]).wait_recv()
        net = inc_ref[s].astype(jnp.float32) - root_field[s]
        total = jnp.concatenate(
            [solve(net[r * size:(r + 1) * size], r) for r in range(row_blocks)], axis=0)
        for l in range(s - 1, -1, -1):
            if l == 0:
                away = slabs.at[s - 1, pl.ds(0, points - rows)]
                to(other, away, away, sx.at[s - 1, 0], rx.at[s - 1]).wait_recv()
            total -= mk_ref[l:l + 1, :] * split_dot(solved_pair[l], slabs[s - 1 - l])
        if s < BACK:
            slabs[s, span(mine, rows), :] = total.astype(jnp.bfloat16)
            for copy in copies_x(s):
                copy.start()
        full[s] = total

        def hand(j, carry):
            copy4(s, j).start()
            return carry

        lax.fori_loop(1, n, hand, 0)
        for unused, copy in copies5(s):
            copy.start()
        for unused, copy in copies6(s):
            copy.start()

    def spread(s):
        to(other, full.at[s, share], full.at[s, share], s4.at[s], r4.at[s]).wait_recv()
        for peer, copy in copies5(s):
            @pl.when(peer != 0)
            def _(copy=copy):
                copy.start()
        away = full.at[s, pl.ds(0, (groups - 1) * thin)]
        to(other, away, away, s5.at[s, 0], r5.at[s]).wait_recv()
        for peer, copy in copies6(s):
            @pl.when(peer != 0)
            def _(copy=copy):
                copy.start()

    local_part(0)
    pl.semaphore_wait(barrier, n + n_pts - 2)
    reduce1(0)
    for s in range(1, STEPS):
        local_part(s)
        reduce1(s)

    @pl.when(is_root)
    def _():
        solve_pairs()

    reduce2(0)
    reduce2(1)
    reduce3(0)
    for s in range(STEPS):
        @pl.when(is_root)
        def _(s=s):
            march(s)

        if s + 2 < STEPS:
            reduce2(s + 2)
        if s + 1 < STEPS:
            reduce3(s + 1)

    @pl.when(jnp.logical_not(is_root))
    def _():
        for s in range(STEPS):
            spread(s)
        for s in range(STEPS):
            away = full.at[s, pl.ds(0, (group - 1) * wide)]
            to(other, away, away, s6.at[s, 0], r6.at[s]).wait_recv()

    out_ref[...] = full[...]

    for s in range(STEPS):
        for copy in copies1(s):
            copy.wait_send()
        for copy in copies2(s):
            copy.wait_send()

        @pl.when(is_root)
        def _(s=s):
            if s < BACK:
                for copy in copies_x(s):
                    copy.wait_send()
            rest = full.at[s, pl.ds(thin, rows - thin)]
            to(other, rest, rest, s4.at[s], r4.at[s]).wait_send()

        @pl.when(jnp.logical_not(is_root))
        def _(s=s):
            copy3(s).wait_send()

        for peer, copy in [*copies5(s), *copies6(s)]:
            @pl.when(jnp.logical_or(is_root, peer != 0))
            def _(copy=copy):
                copy.wait_send()


def per_device(
    n, n_pts, history, incident, kernel_blocks, block_row, block_col, lag_offset, mode_kernel,
    self_inverse,
):
    lags, points, modes = history.shape
    entries, size = kernel_blocks.shape[0], kernel_blocks.shape[1]
    rows = self_inverse.shape[0]
    f32, bf16 = jnp.float32, jnp.bfloat16
    vmem = pl.BlockSpec(memory_space=pltpu.VMEM)
    smem = pl.BlockSpec(memory_space=pltpu.SMEM)
    chunks = 8
    chunk = entries // chunks

    halo = lax.ppermute(history[lags - BACK:], "lag", [(i, i + 1) for i in range(n - 1)])

    part, pair = pl.pallas_call(
        functools.partial(history_kernel, chunk),
        grid=(chunks,),
        out_shape=(
            jax.ShapeDtypeStruct((STEPS, rows, modes), f32),
            jax.ShapeDtypeStruct((BACK, 2 * rows, points), bf16),
        ),
        in_specs=[
            smem, smem, smem,
            pl.BlockSpec((chunk, size, size), lambda i: (i, 0, 0)),
            vmem, vmem,
        ],
        out_specs=(vmem, vmem),
        scratch_shapes=[
            pltpu.VMEM((lags, rows, points), f32),
            pltpu.VMEM((lags, rows, points), f32),
            pltpu.VMEM((2 * rows, points), bf16),
        ],
        compiler_params=pltpu.CompilerParams(vmem_limit_bytes=VMEM_BYTES),
        cost_estimate=pl.CostEstimate(
            flops=4 * lags * rows * points * STEPS * modes,
            bytes_accessed=entries * size * size * 2 + lags * points * modes * 2,
            transcendentals=0),
    )(block_row, block_col, lag_offset, kernel_blocks, history, mode_kernel)

    group = 4 if n % 4 == 0 else 1
    groups = n // group
    wide, thin = rows // group, rows // n
    dma = pltpu.SemaphoreType.DMA
    peers, tops, sides = max(group - 1, 1), max(groups - 1, 1), max(n_pts - 1, 1)
    return pl.pallas_call(
        functools.partial(march_kernel, n, group, groups, n_pts),
        out_shape=jax.ShapeDtypeStruct((STEPS, rows, modes), f32),
        in_specs=[vmem] * 6,
        out_specs=vmem,
        scratch_shapes=[
            pltpu.VMEM((STEPS, rows, modes), f32),
            pltpu.VMEM((STEPS, peers, wide, modes), f32),
            pltpu.VMEM((STEPS, wide, modes), f32),
            pltpu.VMEM((STEPS, tops, thin, modes), f32),
            pltpu.VMEM((STEPS, thin, modes), f32),
            pltpu.VMEM((STEPS, rows, modes), f32),
            pltpu.VMEM((BACK, 2 * rows, points), bf16),
            pltpu.VMEM((BACK, points, modes), bf16),
            pltpu.VMEM((STEPS, rows, modes), f32),
            dma((STEPS, peers)), dma((STEPS,)),
            dma((STEPS, tops)), dma((STEPS,)),
            dma((STEPS,)), dma((STEPS,)),
            dma((STEPS,)), dma((STEPS,)),
            dma((STEPS, tops)), dma((STEPS,)),
            dma((STEPS, peers)), dma((STEPS,)),
            dma((BACK, sides)), dma((BACK,)),
        ],
        compiler_params=pltpu.CompilerParams(
            collective_id=0, has_side_effects=True, vmem_limit_bytes=VMEM_BYTES),
    )(part, pair, halo, mode_kernel, incident, self_inverse)


def solution(mesh):
    return jax.shard_map(
        functools.partial(per_device, mesh.shape["lag"], mesh.shape["pts"]),
        mesh=mesh,
        in_specs=(
            P("lag", None, None),
            P(None, "pts", None),
            P(("lag", "pts"), None, None),
            P(("lag", "pts")),
            P(("lag", "pts")),
            P(("lag", "pts")),
            P("lag", None),
            P("pts", None),
        ),
        out_specs=P(None, "pts", None),
        check_vma=False,
    )
```

```python
import functools
import jax
import jax.numpy as jnp
from jax import lax
from jax.experimental import pallas as pl
from jax.experimental.pallas import tpu as pltpu
from jax.sharding import PartitionSpec as P

STEPS = 4
BACK = STEPS - 1
MESH = pl.DeviceIdType.MESH
VMEM_BYTES = 56 * 1024 * 1024


def split_dot(pair, x):
    both = jnp.dot(pair, x, preferred_element_type=jnp.float32)
    half = both.shape[0] // 2
    return both[:half] + both[half:]


def split_rows(value):
    head = value.astype(jnp.bfloat16)
    rest = (value - head.astype(jnp.float32)).astype(jnp.bfloat16)
    return head, rest


def history_kernel(
    chunks, row_hbm, col_hbm, lag_hbm, k_hbm, hist_hbm, mk_hbm, part_ref, pair_ref,
    even, odd, work, row_ref, col_ref, lag_ref, k_ref, hist_ref, mk_ref, sem, k_sem,
):
    lags, rows, points = even.shape
    entries, size = k_ref.shape[0], k_ref.shape[1]
    modes = hist_ref.shape[2]
    chunk = entries // chunks
    pairs = [(row_hbm, row_ref), (col_hbm, col_ref), (lag_hbm, lag_ref),
             (hist_hbm, hist_ref), (mk_hbm, mk_ref)]
    loads = [pltpu.make_async_copy(src, dst, sem.at[i]) for i, (src, dst) in enumerate(pairs)]

    def load_k(c):
        span = pl.ds(c * chunk, chunk)
        return pltpu.make_async_copy(k_hbm.at[span], k_ref.at[span], k_sem.at[c])

    for copy in loads[:3]:
        copy.start()
    for c in range(chunks):
        load_k(c).start()
    for copy in loads[3:]:
        copy.start()
    even[...] = jnp.zeros_like(even)
    odd[...] = jnp.zeros_like(odd)
    for copy in loads[:3]:
        copy.wait()

    def add(total, e):
        r = pl.multiple_of(row_ref[e] * size, size)
        c = pl.multiple_of(col_ref[e] * size, size)
        total[lag_ref[e], pl.ds(r, size), pl.ds(c, size)] += k_ref[e].astype(jnp.float32)

    def take(c, carry):
        load_k(c).wait()

        def body(j, carry):
            add(even, c * chunk + 2 * j)
            add(odd, c * chunk + 2 * j + 1)
            return carry

        return lax.fori_loop(0, chunk // 2, body, carry, unroll=2)

    lax.fori_loop(0, chunks, take, 0)
    for copy in loads[3:]:
        copy.wait()
    for l in range(lags):
        head, rest = split_rows(even[l] + odd[l])
        target = pair_ref.at[l] if l < BACK else work
        target[:rows, :] = head
        target[rows:, :] = rest
        count = min(l, BACK) + 1
        x = jnp.concatenate([hist_ref[l - s] for s in range(count)], axis=1)
        found = split_dot(target[...], x)
        for s in range(count):
            term = found[:, s * modes:(s + 1) * modes] * mk_ref[l:l + 1, :]
            if l == s:
                part_ref[s] = term
            else:
                part_ref[s] += term


def march_kernel(
    n, group, groups, n_pts,
    part_ref, pair_ref, hist_hbm, mk_ref, inc_ref, inv_ref, out_ref,
    halo_ref, inv_pair, field, got1, sum1, got2, sum2, root_field, solved_pair, slabs, full,
    s1, r1, s2, r2, s3, r3, s4, r4, s5, r5, s6, r6, s7, r7, s8, sx, rx, sh, rh,
):
    me = lax.axis_index("lag")
    mine = lax.axis_index("pts")
    g = lax.rem(me, group)
    z = me // group
    rows = part_ref.shape[1]
    modes = part_ref.shape[2]
    points = halo_ref.shape[1]
    size = inv_ref.shape[1]
    row_blocks = rows // size
    wide = rows // group
    thin = rows // n
    is_root = me == 0
    lags = hist_hbm.shape[0]
    hubs = [1 if s < BACK and group > 1 else 0 for s in range(STEPS)]

    barrier = pltpu.get_barrier_semaphore()

    def greet(k, carry):
        pl.semaphore_signal(
            barrier, inc=1, device_id={"lag": lax.rem(me + k, n)}, device_id_type=MESH
        )
        return carry

    lax.fori_loop(1, n, greet, 0)

    for k in range(1, n_pts):
        pl.semaphore_signal(
            barrier, inc=1, device_id={"pts": lax.rem(mine + k, n_pts)}, device_id_type=MESH
        )

    def to(device, src, dst, send, recv):
        return pltpu.make_async_remote_copy(
            src_ref=src, dst_ref=dst, send_sem=send, recv_sem=recv,
            device_id=device, device_id_type=MESH,
        )

    def in_group(k):
        return lax.rem(g + k, group)

    def in_column(k):
        return lax.rem(z + k, groups)

    def span(first, count):
        return pl.ds(pl.multiple_of(first * count, count), count)

    other = {"lag": lax.rem(me + 1, n)}

    def copies1(s):
        for k in range(1, group):
            peer = in_group(k)
            yield to({"lag": z * group + peer}, field.at[s, span(peer, wide)],
                     got1.at[s, k - 1], s1.at[s, k - 1], r1.at[s])

    def copies2(s):
        for k in range(1, groups):
            peer = in_column(k)
            yield to({"lag": peer * group + g}, sum1.at[s, span(peer, thin)],
                     got2.at[s, k - 1], s2.at[s, k - 1], r2.at[s])

    share = span(g * groups + z, thin)

    def copy3(s):
        return to({"lag": 0}, sum2.at[s], root_field.at[s, share], s3.at[s], r3.at[s])

    def halo_copy(i):
        return to({"lag": lax.rem(me + 1, n)}, hist_hbm.at[lags - BACK + i], halo_ref.at[i],
                  sh.at[i], rh.at[i])

    def local_part(s):
        halo_copy(BACK - s).wait_recv()
        total = part_ref[s]
        for l in range(s):
            total += mk_ref[l:l + 1, :] * split_dot(pair_ref[l], halo_ref[BACK + l - s])
        field[s] = total

    def reduce1(s):
        for copy in copies1(s):
            copy.start()

    def reduce2(s):
        to(other, got1.at[s], got1.at[s], s1.at[s, 0], r1.at[s]).wait_recv()
        total = field[s, span(g, wide), :]
        for k in range(group - 1):
            total += got1[s, k]
        sum1[s] = total
        for copy in copies2(s):
            copy.start()

    def reduce3(s):
        to(other, got2.at[s], got2.at[s], s2.at[s, 0], r2.at[s]).wait_recv()
        total = sum1[s, span(z, thin), :]
        for k in range(groups - 1):
            total += got2[s, k]

        @pl.when(is_root)
        def _():
            root_field[s, 0:thin, :] = total

        @pl.when(jnp.logical_not(is_root))
        def _():
            sum2[s] = total
            copy3(s).start()

    def solve(head, rest, r):
        both = jnp.dot(inv_pair[r], head, preferred_element_type=jnp.float32)
        last = jnp.dot(inv_pair[r, :size, :], rest, preferred_element_type=jnp.float32)
        return both[:size] + both[size:] + last

    def solve_pair(l):
        for r in range(row_blocks):
            block = slice(r * size, (r + 1) * size)
            below = slice(rows + r * size, rows + (r + 1) * size)
            head, rest = split_rows(solve(pair_ref[l, block, :], pair_ref[l, below, :], r))
            solved_pair[l, block, :] = head
            solved_pair[l, below, :] = rest

    def copies_x(s):
        for k in range(1, n_pts):
            here = slabs.at[s, span(mine, rows)]
            yield to({"pts": lax.rem(mine + k, n_pts)}, here, here, sx.at[s, k - 1], rx.at[s])

    def copy4(s, j):
        part = span(lax.rem(j, group) * groups + j // group, thin)
        return to({"lag": j}, full.at[s, part], full.at[s, part], s4.at[s], r4.at[s])

    def copies5(s):
        for k in range(1, groups):
            peer = in_column(k) * group + g
            here = full.at[s, share]
            yield peer, to({"lag": peer}, here, here, s5.at[s, k - 1], r5.at[s])

    def copies6(s):
        for k in range(1, group):
            peer = z * group + in_group(k)
            here = full.at[s, span(g, wide)]
            yield peer, to({"lag": peer}, here, here, s6.at[s, k - 1], r6.at[s])

    def copies_for_root(s):
        here = full.at[s, pl.ds(0, thin)]
        for k in range(1, groups):
            yield to({"lag": k * group}, here, here, s8.at[s, k - 1], r5.at[s])
        here = full.at[s, pl.ds(0, wide)]
        for k in range(2, group):
            yield to({"lag": k}, here, here, s8.at[s, groups + k - 3], r6.at[s])

    def copy7(s):
        return to({"lag": hubs[s]}, full.at[s], full.at[s], s7.at[s], r7.at[s])

    def needs(s, peer):
        if hubs[s] == 0:
            return peer != 0
        return jnp.logical_and(peer != 0, peer != hubs[s])

    def hand_out(s):
        hub = hubs[s]

        def hand(j, carry):
            copy4(s, j).start()
            return carry

        lax.fori_loop(hub + 1, n, hand, 0)
        for peer, copy in [*copies5(s), *copies6(s)]:
            if hub == 0:
                copy.start()
            else:
                @pl.when(peer != 0)
                def _(copy=copy):
                    copy.start()
        if hub != 0:
            for copy in copies_for_root(s):
                copy.start()

    def march(s):
        if s > 0:
            rest = root_field.at[s, pl.ds(thin, rows - thin)]
            to(other, rest, rest, s3.at[s], r3.at[s]).wait_recv()
        net = inc_ref[s].astype(jnp.float32) - root_field[s]
        blocks = [split_rows(net[r * size:(r + 1) * size]) for r in range(row_blocks)]
        total = jnp.concatenate(
            [solve(head, rest, r) for r, (head, rest) in enumerate(blocks)], axis=0)
        for l in range(s - 1, -1, -1):
            if l == 0:
                away = slabs.at[s - 1, pl.ds(0, points - rows)]
                to(other, away, away, sx.at[s - 1, 0], rx.at[s - 1]).wait_recv()
            total -= mk_ref[l:l + 1, :] * split_dot(solved_pair[l], slabs[s - 1 - l])
        if s < BACK:
            slabs[s, span(mine, rows), :] = total.astype(jnp.bfloat16)
            for copy in copies_x(s):
                copy.start()
        full[s] = total
        if hubs[s] == 0:
            hand_out(s)
        else:
            copy7(s).start()

    def pass_on(s):
        def plain():
            to(other, full.at[s, share], full.at[s, share], s4.at[s], r4.at[s]).wait_recv()
            for peer, copy in copies5(s):
                @pl.when(needs(s, peer))
                def _(copy=copy):
                    copy.start()

        if hubs[s] == 0:
            plain()
        else:
            @pl.when(me == hubs[s])
            def _():
                copy7(s).wait_recv()
                hand_out(s)

            pl.when(me != hubs[s])(plain)

    def fill(s):
        def plain():
            away = full.at[s, pl.ds(0, (groups - 1) * thin)]
            to(other, away, away, s5.at[s, 0], r5.at[s]).wait_recv()
            for peer, copy in copies6(s):
                @pl.when(needs(s, peer))
                def _(copy=copy):
                    copy.start()

        if hubs[s] == 0:
            plain()
        else:
            pl.when(me != hubs[s])(plain)

    def finish(s):
        def plain():
            away = full.at[s, pl.ds(0, (group - 1) * wide)]
            to(other, away, away, s6.at[s, 0], r6.at[s]).wait_recv()

        if hubs[s] == 0:
            plain()
        else:
            pl.when(me != hubs[s])(plain)

    field[0] = part_ref[0]

    @pl.when(is_root)
    def _():
        for s in range(1, STEPS):
            field[s] = part_ref[s]
        for r in range(row_blocks):
            head, rest = split_rows(inv_ref[r * size:(r + 1) * size, :])
            inv_pair[r, :size, :] = head
            inv_pair[r, size:, :] = rest

    pl.semaphore_wait(barrier, n + n_pts - 2)
    reduce1(0)

    @pl.when(me < n - 1)
    def _():
        for i in range(BACK - 1, -1, -1):
            halo_copy(i).start()

    @pl.when(is_root)
    def _():
        for s in range(1, STEPS):
            reduce1(s)
        for l in range(BACK):
            solve_pair(l)
        reduce2(0)
        reduce3(0)
        rest = root_field.at[0, pl.ds(thin, rows - thin)]
        to(other, rest, rest, s3.at[0], r3.at[0]).wait_recv()
        reduce2(1)
        march(0)
        for s in range(1, STEPS):
            reduce3(s)
            if s + 1 < STEPS:
                reduce2(s + 1)
            march(s)

    @pl.when(jnp.logical_not(is_root))
    def _():
        reduce2(0)
        local_part(1)
        reduce1(1)
        reduce3(0)
        local_part(2)
        reduce1(2)
        reduce2(1)
        local_part(3)
        reduce1(3)
        reduce3(1)
        reduce2(2)
        reduce3(2)
        reduce2(3)
        reduce3(3)
        pass_on(0)
        pass_on(1)
        fill(0)
        pass_on(2)
        fill(1)
        fill(2)
        pass_on(3)
        fill(3)
        for s in range(STEPS):
            finish(s)

    out_ref[...] = full[...]

    @pl.when(me < n - 1)
    def _():
        for i in range(BACK):
            halo_copy(i).wait_send()

    for s in range(STEPS):
        hub = hubs[s]
        for copy in copies1(s):
            copy.wait_send()
        for copy in copies2(s):
            copy.wait_send()

        @pl.when(is_root)
        def _(s=s, hub=hub):
            if s < BACK:
                for copy in copies_x(s):
                    copy.wait_send()
            if hub != 0:
                copy7(s).wait_send()

        @pl.when(jnp.logical_not(is_root))
        def _(s=s):
            copy3(s).wait_send()

        @pl.when(me == hub)
        def _(s=s, hub=hub):
            rest = full.at[s, pl.ds(0, (n - 1 - hub) * thin)]
            to(other, rest, rest, s4.at[s], r4.at[s]).wait_send()
            if hub != 0:
                for copy in copies_for_root(s):
                    copy.wait_send()

        for peer, copy in [*copies5(s), *copies6(s)]:
            if hub == 0:
                sent = jnp.logical_or(is_root, peer != 0)
            else:
                sent = jnp.logical_and(
                    jnp.logical_not(is_root),
                    jnp.logical_and(peer != 0, jnp.logical_or(me == hub, peer != hub)))

            @pl.when(sent)
            def _(copy=copy):
                copy.wait_send()


def per_device(
    n, n_pts, history, incident, kernel_blocks, block_row, block_col, lag_offset, mode_kernel,
    self_inverse,
):
    lags, points, modes = history.shape
    entries, size = kernel_blocks.shape[0], kernel_blocks.shape[1]
    rows = self_inverse.shape[0]
    f32, bf16 = jnp.float32, jnp.bfloat16
    vmem = pl.BlockSpec(memory_space=pltpu.VMEM)
    hbm = pl.BlockSpec(memory_space=pltpu.HBM)
    chunks = 8
    dma = pltpu.SemaphoreType.DMA

    part, pair = pl.pallas_call(
        functools.partial(history_kernel, chunks),
        out_shape=(
            jax.ShapeDtypeStruct((STEPS, rows, modes), f32),
            jax.ShapeDtypeStruct((BACK, 2 * rows, points), bf16),
        ),
        in_specs=[hbm] * 6,
        out_specs=(vmem, vmem),
        scratch_shapes=[
            pltpu.VMEM((lags, rows, points), f32),
            pltpu.VMEM((lags, rows, points), f32),
            pltpu.VMEM((2 * rows, points), bf16),
            pltpu.SMEM((entries,), jnp.int32),
            pltpu.SMEM((entries,), jnp.int32),
            pltpu.SMEM((entries,), jnp.int32),
            pltpu.VMEM((entries, size, size), bf16),
            pltpu.VMEM((lags, points, modes), bf16),
            pltpu.VMEM((lags, modes), f32),
            dma((5,)), dma((chunks,)),
        ],
        compiler_params=pltpu.CompilerParams(vmem_limit_bytes=VMEM_BYTES),
    )(block_row, block_col, lag_offset, kernel_blocks, history, mode_kernel)

    group = 4 if n % 4 == 0 else 1
    groups = n // group
    wide, thin = rows // group, rows // n
    peers, tops, sides = max(group - 1, 1), max(groups - 1, 1), max(n_pts - 1, 1)
    return pl.pallas_call(
        functools.partial(march_kernel, n, group, groups, n_pts),
        out_shape=jax.ShapeDtypeStruct((STEPS, rows, modes), f32),
        in_specs=[vmem, vmem, hbm, vmem, vmem, vmem],
        out_specs=vmem,
        scratch_shapes=[
            pltpu.VMEM((BACK, points, modes), bf16),
            pltpu.VMEM((rows // size, 2 * size, size), bf16),
            pltpu.VMEM((STEPS, rows, modes), f32),
            pltpu.VMEM((STEPS, peers, wide, modes), f32),
            pltpu.VMEM((STEPS, wide, modes), f32),
            pltpu.VMEM((STEPS, tops, thin, modes), f32),
            pltpu.VMEM((STEPS, thin, modes), f32),
            pltpu.VMEM((STEPS, rows, modes), f32),
            pltpu.VMEM((BACK, 2 * rows, points), bf16),
            pltpu.VMEM((BACK, points, modes), bf16),
            pltpu.VMEM((STEPS, rows, modes), f32),
            dma((STEPS, peers)), dma((STEPS,)),
            dma((STEPS, tops)), dma((STEPS,)),
            dma((STEPS,)), dma((STEPS,)),
            dma((STEPS,)), dma((STEPS,)),
            dma((STEPS, tops)), dma((STEPS,)),
            dma((STEPS, peers)), dma((STEPS,)),
            dma((STEPS,)), dma((STEPS,)), dma((STEPS, tops + peers)),
            dma((BACK, sides)), dma((BACK,)),
            dma((BACK,)), dma((BACK,)),
        ],
        compiler_params=pltpu.CompilerParams(
            collective_id=0, has_side_effects=True, vmem_limit_bytes=VMEM_BYTES),
    )(part, pair, history, mode_kernel, incident, self_inverse)


def solution(mesh):
    return jax.shard_map(
        functools.partial(per_device, mesh.shape["lag"], mesh.shape["pts"]),
        mesh=mesh,
        in_specs=(
            P("lag", None, None),
            P(None, "pts", None),
            P(("lag", "pts"), None, None),
            P(("lag", "pts")),
            P(("lag", "pts")),
            P(("lag", "pts")),
            P("lag", None),
            P("pts", None),
        ),
        out_specs=P(None, "pts", None),
        check_vma=False,
    )
```

```python
import functools
import jax
import jax.numpy as jnp
from jax import lax
from jax.experimental import pallas as pl
from jax.experimental.pallas import tpu as pltpu
from jax.sharding import PartitionSpec as P

STEPS = 4
BACK = STEPS - 1
MESH = pl.DeviceIdType.MESH


def split_dot(pair, x):
    both = jnp.dot(pair, x, preferred_element_type=jnp.float32)
    half = both.shape[0] // 2
    return both[:half] + both[half:]


def split_rows(value):
    head = value.astype(jnp.bfloat16)
    rest = (value - head.astype(jnp.float32)).astype(jnp.bfloat16)
    return head, rest


def history_kernel(
    chunks, row_hbm, col_hbm, lag_hbm, k_hbm, hist_hbm, mk_hbm, part_ref, pair_ref,
    even, odd, work, row_ref, col_ref, lag_ref, k_ref, hist_ref, mk_ref, sem, k_sem,
):
    lags, rows, points = even.shape
    entries, size = k_ref.shape[0], k_ref.shape[1]
    modes = hist_ref.shape[2]
    chunk = entries // chunks
    pairs = [(row_hbm, row_ref), (col_hbm, col_ref), (lag_hbm, lag_ref),
             (hist_hbm, hist_ref), (mk_hbm, mk_ref)]
    loads = [pltpu.make_async_copy(src, dst, sem.at[i]) for i, (src, dst) in enumerate(pairs)]

    def load_k(c):
        span = pl.ds(c * chunk, chunk)
        return pltpu.make_async_copy(k_hbm.at[span], k_ref.at[span], k_sem.at[c])

    for copy in loads[:3]:
        copy.start()
    for c in range(chunks):
        load_k(c).start()
    for copy in loads[3:]:
        copy.start()
    even[...] = jnp.zeros_like(even)
    odd[...] = jnp.zeros_like(odd)
    for copy in loads[:3]:
        copy.wait()

    def add(total, e):
        r = pl.multiple_of(row_ref[e] * size, size)
        c = pl.multiple_of(col_ref[e] * size, size)
        total[lag_ref[e], pl.ds(r, size), pl.ds(c, size)] += k_ref[e].astype(jnp.float32)

    def take(c, carry):
        load_k(c).wait()

        def body(j, carry):
            add(even, c * chunk + 2 * j)
            add(odd, c * chunk + 2 * j + 1)
            return carry

        return lax.fori_loop(0, chunk // 2, body, carry, unroll=2)

    lax.fori_loop(0, chunks, take, 0)
    for copy in loads[3:]:
        copy.wait()
    for l in range(lags):
        head, rest = split_rows(even[l] + odd[l])
        target = pair_ref.at[l] if l < BACK else work
        target[:rows, :] = head
        target[rows:, :] = rest
        count = min(l, BACK) + 1
        x = jnp.concatenate([hist_ref[l - s] for s in range(count)], axis=1)
        found = split_dot(target[...], x)
        for s in range(count):
            term = found[:, s * modes:(s + 1) * modes] * mk_ref[l:l + 1, :]
            if l == s:
                part_ref[s] = term
            else:
                part_ref[s] += term


def march_kernel(
    n, n_pts,
    part_ref, pair_ref, hist_hbm, mk_ref, inc_ref, inv_ref, out_ref,
    halo_ref, inv_pair, field, got_c, sum_c, got_x, sum_x, got_z, sum_z,
    root_field, solved_pair, slabs, full,
    sc, rc, sw, rw, s2, r2, s3, r3, s4, r4, s5, r5, s6, r6, s7, r7, s8, s9, r9, sx, rx, sh, rh,
):
    me = lax.axis_index("lag")
    mine = lax.axis_index("pts")
    core = lax.rem(me, 2)
    side = lax.rem(me // 2, 2)
    z = me // 4
    groups = n // 4
    quarter = core * 2 + side
    sibling = {"lag": me + 1 - 2 * core}
    across = {"lag": me + 2 - 4 * side}
    rows = part_ref.shape[1]
    modes = part_ref.shape[2]
    points = halo_ref.shape[1]
    size = inv_ref.shape[1]
    row_blocks = rows // size
    half = rows // 2
    wide = rows // 4
    thin = rows // n
    is_root = me == 0
    lags = hist_hbm.shape[0]
    hubs = [1 if s < BACK else 0 for s in range(STEPS)]

    barrier = pltpu.get_barrier_semaphore()

    def greet(k, carry):
        pl.semaphore_signal(
            barrier, inc=1, device_id={"lag": lax.rem(me + k, n)}, device_id_type=MESH
        )
        return carry

    lax.fori_loop(1, n, greet, 0)

    for k in range(1, n_pts):
        pl.semaphore_signal(
            barrier, inc=1, device_id={"pts": lax.rem(mine + k, n_pts)}, device_id_type=MESH
        )

    def to(device, src, dst, send, recv):
        return pltpu.make_async_remote_copy(
            src_ref=src, dst_ref=dst, send_sem=send, recv_sem=recv,
            device_id=device, device_id_type=MESH,
        )

    def in_column(k):
        return lax.rem(z + k, groups)

    def span(first, count):
        return pl.ds(pl.multiple_of(first * count, count), count)

    other = {"lag": lax.rem(me + 1, n)}

    def copy_c(s):
        return to(sibling, field.at[s, span(1 - core, half)], got_c.at[s], sc.at[s], rc.at[s])

    def copy_w(s):
        return to(across, sum_c.at[s, span(1 - side, wide)], got_x.at[s], sw.at[s], rw.at[s])

    def copies2(s):
        for k in range(1, groups):
            peer = in_column(k)
            yield to({"lag": peer * 4 + lax.rem(me, 4)}, sum_x.at[s, span(peer, thin)],
                     got_z.at[s, k - 1], s2.at[s, k - 1], r2.at[s])

    share = span(quarter * groups + z, thin)

    def copy3(s):
        return to({"lag": 0}, sum_z.at[s], root_field.at[s, share], s3.at[s], r3.at[s])

    def halo_copy(i):
        return to({"lag": lax.rem(me + 1, n)}, hist_hbm.at[lags - BACK + i], halo_ref.at[i],
                  sh.at[i], rh.at[i])

    def local_part(s):
        halo_copy(BACK - s).wait_recv()
        total = part_ref[s]
        for l in range(s):
            total += mk_ref[l:l + 1, :] * split_dot(pair_ref[l], halo_ref[BACK + l - s])
        field[s] = total

    def reduce_c(s):
        copy_c(s).start()

    def reduce_x(s):
        copy_c(s).wait_recv()
        sum_c[s] = field[s, span(core, half), :] + got_c[s]
        copy_w(s).start()

    def reduce_z(s):
        copy_w(s).wait_recv()
        sum_x[s] = sum_c[s, span(side, wide), :] + got_x[s]
        for copy in copies2(s):
            copy.start()

    def reduce3(s):
        to(other, got_z.at[s], got_z.at[s], s2.at[s, 0], r2.at[s]).wait_recv()
        total = sum_x[s, span(z, thin), :]
        for k in range(groups - 1):
            total += got_z[s, k]

        @pl.when(is_root)
        def _():
            root_field[s, 0:thin, :] = total

        @pl.when(jnp.logical_not(is_root))
        def _():
            sum_z[s] = total
            copy3(s).start()

    def solve(head, rest, r):
        both = jnp.dot(inv_pair[r], head, preferred_element_type=jnp.float32)
        last = jnp.dot(inv_pair[r, :size, :], rest, preferred_element_type=jnp.float32)
        return both[:size] + both[size:] + last

    def solve_pair(l):
        for r in range(row_blocks):
            block = slice(r * size, (r + 1) * size)
            below = slice(rows + r * size, rows + (r + 1) * size)
            head, rest = split_rows(solve(pair_ref[l, block, :], pair_ref[l, below, :], r))
            solved_pair[l, block, :] = head
            solved_pair[l, below, :] = rest

    def copies_x(s):
        for k in range(1, n_pts):
            here = slabs.at[s, span(mine, rows)]
            yield to({"pts": lax.rem(mine + k, n_pts)}, here, here, sx.at[s, k - 1], rx.at[s])

    def copy4(s, j):
        owner = lax.rem(j, 2) * 2 + lax.rem(j // 2, 2)
        part = span(owner * groups + j // 4, thin)
        return to({"lag": j}, full.at[s, part], full.at[s, part], s4.at[s], r4.at[s])

    def copies5(s):
        for k in range(1, groups):
            peer = in_column(k) * 4 + lax.rem(me, 4)
            here = full.at[s, share]
            yield peer, to({"lag": peer}, here, here, s5.at[s, k - 1], r5.at[s])

    def copy6(s):
        here = full.at[s, span(quarter, wide)]
        return to(across, here, here, s6.at[s], r6.at[s])

    def copy9(s):
        here = full.at[s, span(core, half)]
        return to(sibling, here, here, s9.at[s], r9.at[s])

    def copies_for_root(s):
        here = full.at[s, pl.ds(0, thin)]
        for k in range(1, groups):
            yield to({"lag": k * 4}, here, here, s8.at[s, k - 1], r5.at[s])
        here = full.at[s, pl.ds(0, wide)]
        yield to({"lag": 2}, here, here, s8.at[s, groups - 1], r6.at[s])

    def copy7(s):
        return to({"lag": hubs[s]}, full.at[s], full.at[s], s7.at[s], r7.at[s])

    def needs(s, peer):
        if hubs[s] == 0:
            return peer != 0
        return jnp.logical_and(peer != 0, peer != hubs[s])

    def hand_out(s):
        hub = hubs[s]

        def hand(j, carry):
            copy4(s, n + hub - j).start()
            return carry

        lax.fori_loop(hub + 1, n, hand, 0)
        for unused, copy in copies5(s):
            copy.start()
        copy6(s).start()
        if hub == 0:
            copy9(s).start()
        else:
            for copy in copies_for_root(s):
                copy.start()

    def march(s):
        if s > 0:
            rest = root_field.at[s, pl.ds(thin, rows - thin)]
            to(other, rest, rest, s3.at[s], r3.at[s]).wait_recv()
        net = inc_ref[s].astype(jnp.float32) - root_field[s]
        blocks = [split_rows(net[r * size:(r + 1) * size]) for r in range(row_blocks)]
        total = jnp.concatenate(
            [solve(head, rest, r) for r, (head, rest) in enumerate(blocks)], axis=0)
        for l in range(s - 1, -1, -1):
            if l == 0:
                away = slabs.at[s - 1, pl.ds(0, points - rows)]
                to(other, away, away, sx.at[s - 1, 0], rx.at[s - 1]).wait_recv()
            total -= mk_ref[l:l + 1, :] * split_dot(solved_pair[l], slabs[s - 1 - l])
        if s < BACK:
            slabs[s, span(mine, rows), :] = total.astype(jnp.bfloat16)
            for copy in copies_x(s):
                copy.start()
        full[s] = total
        if hubs[s] == 0:
            hand_out(s)
        else:
            copy7(s).start()

    def pass_on(s):
        def plain():
            to(other, full.at[s, share], full.at[s, share], s4.at[s], r4.at[s]).wait_recv()
            for peer, copy in copies5(s):
                @pl.when(needs(s, peer))
                def _(copy=copy):
                    copy.start()

        if hubs[s] == 0:
            plain()
        else:
            @pl.when(me == hubs[s])
            def _():
                copy7(s).wait_recv()
                hand_out(s)

            pl.when(me != hubs[s])(plain)

    def unless_hub(s, act):
        if hubs[s] == 0:
            act()
        else:
            pl.when(me != hubs[s])(act)

    def fill_x(s):
        def act():
            away = full.at[s, pl.ds(0, (groups - 1) * thin)]
            to(other, away, away, s5.at[s, 0], r5.at[s]).wait_recv()

            @pl.when(needs(s, across["lag"]))
            def _():
                copy6(s).start()

        unless_hub(s, act)

    def fill_c(s):
        def act():
            copy6(s).wait_recv()

            @pl.when(needs(s, sibling["lag"]))
            def _():
                copy9(s).start()

        unless_hub(s, act)

    def finish(s):
        unless_hub(s, lambda: copy9(s).wait_recv())

    field[0] = part_ref[0]

    @pl.when(is_root)
    def _():
        for s in range(1, STEPS):
            field[s] = part_ref[s]
        for r in range(row_blocks):
            head, rest = split_rows(inv_ref[r * size:(r + 1) * size, :])
            inv_pair[r, :size, :] = head
            inv_pair[r, size:, :] = rest

    pl.semaphore_wait(barrier, n + n_pts - 2)
    reduce_c(0)

    def send_halo():
        @pl.when(me < n - 1)
        def _():
            for i in range(BACK - 1, -1, -1):
                halo_copy(i).start()

    @pl.when(is_root)
    def _():
        solve_pair(0)
        reduce_x(0)
        send_halo()
        for s in range(1, STEPS):
            reduce_c(s)
        reduce_z(0)
        reduce_x(1)
        reduce3(0)
        rest = root_field.at[0, pl.ds(thin, rows - thin)]
        to(other, rest, rest, s3.at[0], r3.at[0]).wait_recv()
        march(0)
        reduce_z(1)
        reduce_x(2)
        solve_pair(1)
        reduce3(1)
        reduce_z(2)
        reduce_x(3)
        march(1)
        solve_pair(2)
        reduce3(2)
        reduce_z(3)
        march(2)
        reduce3(3)
        march(3)

    @pl.when(jnp.logical_not(is_root))
    def _():
        reduce_x(0)
        send_halo()
        reduce_z(0)
        local_part(1)
        reduce_c(1)
        reduce3(0)
        reduce_x(1)
        local_part(2)
        reduce_c(2)
        reduce_z(1)
        reduce_x(2)
        local_part(3)
        reduce_c(3)
        reduce3(1)
        reduce_z(2)
        reduce_x(3)
        reduce3(2)
        reduce_z(3)
        reduce3(3)
        pass_on(0)
        pass_on(1)
        fill_x(0)
        pass_on(2)
        fill_x(1)
        fill_c(0)
        fill_x(2)
        fill_c(1)
        fill_c(2)
        pass_on(3)
        fill_x(3)
        fill_c(3)
        for s in range(STEPS):
            finish(s)

    out_ref[...] = full[...]

    @pl.when(me < n - 1)
    def _():
        for i in range(BACK):
            halo_copy(i).wait_send()

    for s in range(STEPS):
        hub = hubs[s]
        copy_c(s).wait_send()
        copy_w(s).wait_send()
        for copy in copies2(s):
            copy.wait_send()

        @pl.when(is_root)
        def _(s=s, hub=hub):
            if s < BACK:
                for copy in copies_x(s):
                    copy.wait_send()
            if hub != 0:
                copy7(s).wait_send()

        @pl.when(jnp.logical_not(is_root))
        def _(s=s):
            copy3(s).wait_send()

        @pl.when(me == hub)
        def _(s=s, hub=hub):
            rest = full.at[s, pl.ds(0, (n - 1 - hub) * thin)]
            to(other, rest, rest, s4.at[s], r4.at[s]).wait_send()
            if hub != 0:
                for copy in copies_for_root(s):
                    copy.wait_send()

        chain = [(across["lag"], copy6(s))]
        if hub == 0:
            chain.append((sibling["lag"], copy9(s)))
        else:
            @pl.when(jnp.logical_and(me > hub, needs(s, sibling["lag"])))
            def _(s=s):
                copy9(s).wait_send()
        for peer, copy in [*copies5(s), *chain]:
            if hub == 0:
                sent = jnp.logical_or(is_root, peer != 0)
            else:
                sent = jnp.logical_and(
                    jnp.logical_not(is_root),
                    jnp.logical_and(peer != 0, jnp.logical_or(me == hub, peer != hub)))

            @pl.when(sent)
            def _(copy=copy):
                copy.wait_send()


def per_device(
    n, n_pts, history, incident, kernel_blocks, block_row, block_col, lag_offset, mode_kernel,
    self_inverse,
):
    lags, points, modes = history.shape
    entries, size = kernel_blocks.shape[0], kernel_blocks.shape[1]
    rows = self_inverse.shape[0]
    f32, bf16 = jnp.float32, jnp.bfloat16
    vmem = pl.BlockSpec(memory_space=pltpu.VMEM)
    hbm = pl.BlockSpec(memory_space=pltpu.HBM)
    chunks = 8
    history_bytes = 6 * 1024 * 1024 + (
        8 * lags * rows * points + 2 * entries * size * size + 2 * lags * points * modes
        + 4 * (BACK + 1) * rows * points)
    dma = pltpu.SemaphoreType.DMA

    part, pair = pl.pallas_call(
        functools.partial(history_kernel, chunks),
        out_shape=(
            jax.ShapeDtypeStruct((STEPS, rows, modes), f32),
            jax.ShapeDtypeStruct((BACK, 2 * rows, points), bf16),
        ),
        in_specs=[hbm] * 6,
        out_specs=(vmem, vmem),
        scratch_shapes=[
            pltpu.VMEM((lags, rows, points), f32),
            pltpu.VMEM((lags, rows, points), f32),
            pltpu.VMEM((2 * rows, points), bf16),
            pltpu.SMEM((entries,), jnp.int32),
            pltpu.SMEM((entries,), jnp.int32),
            pltpu.SMEM((entries,), jnp.int32),
            pltpu.VMEM((entries, size, size), bf16),
            pltpu.VMEM((lags, points, modes), bf16),
            pltpu.VMEM((lags, modes), f32),
            dma((5,)), dma((chunks,)),
        ],
        compiler_params=pltpu.CompilerParams(vmem_limit_bytes=history_bytes),
    )(block_row, block_col, lag_offset, kernel_blocks, history, mode_kernel)

    groups = n // 4
    wide, thin = rows // 4, rows // n
    march_bytes = 8 * 1024 * 1024 + 40 * BACK * rows * points
    tops, sides = max(groups - 1, 1), max(n_pts - 1, 1)
    return pl.pallas_call(
        functools.partial(march_kernel, n, n_pts),
        out_shape=jax.ShapeDtypeStruct((STEPS, rows, modes), f32),
        in_specs=[vmem, vmem, hbm, vmem, vmem, vmem],
        out_specs=vmem,
        scratch_shapes=[
            pltpu.VMEM((BACK, points, modes), bf16),
            pltpu.VMEM((rows // size, 2 * size, size), bf16),
            pltpu.VMEM((STEPS, rows, modes), f32),
            pltpu.VMEM((STEPS, rows // 2, modes), f32),
            pltpu.VMEM((STEPS, rows // 2, modes), f32),
            pltpu.VMEM((STEPS, wide, modes), f32),
            pltpu.VMEM((STEPS, wide, modes), f32),
            pltpu.VMEM((STEPS, tops, thin, modes), f32),
            pltpu.VMEM((STEPS, thin, modes), f32),
            pltpu.VMEM((STEPS, rows, modes), f32),
            pltpu.VMEM((BACK, 2 * rows, points), bf16),
            pltpu.VMEM((BACK, points, modes), bf16),
            pltpu.VMEM((STEPS, rows, modes), f32),
            dma((STEPS,)), dma((STEPS,)), dma((STEPS,)), dma((STEPS,)),
            dma((STEPS, tops)), dma((STEPS,)), dma((STEPS,)), dma((STEPS,)),
            dma((STEPS,)), dma((STEPS,)), dma((STEPS, tops)), dma((STEPS,)),
            dma((STEPS,)), dma((STEPS,)), dma((STEPS,)), dma((STEPS,)),
            dma((STEPS, tops + 1)), dma((STEPS,)), dma((STEPS,)),
            dma((BACK, sides)), dma((BACK,)), dma((BACK,)), dma((BACK,)),
        ],
        compiler_params=pltpu.CompilerParams(
            collective_id=0, has_side_effects=True, vmem_limit_bytes=march_bytes),
    )(part, pair, history, mode_kernel, incident, self_inverse)


def solution(mesh):
    return jax.shard_map(
        functools.partial(per_device, mesh.shape["lag"], mesh.shape["pts"]),
        mesh=mesh,
        in_specs=(
            P("lag", None, None),
            P(None, "pts", None),
            P(("lag", "pts"), None, None),
            P(("lag", "pts")),
            P(("lag", "pts")),
            P(("lag", "pts")),
            P("lag", None),
            P("pts", None),
        ),
        out_specs=P(None, "pts", None),
        check_vma=False,
    )
```

```python
import functools
import jax
import jax.numpy as jnp
from jax import lax
from jax.experimental import pallas as pl
from jax.experimental.pallas import tpu as pltpu
from jax.sharding import PartitionSpec as P

STEPS = 4
BACK = STEPS - 1
HISTORY_BYTES = 50 * 1024 * 1024
MESH = pl.DeviceIdType.MESH


def split_dot(pair, x):
    both = jnp.dot(pair, x, preferred_element_type=jnp.float32)
    half = both.shape[0] // 2
    return both[:half] + both[half:]


def split_rows(value):
    head = value.astype(jnp.bfloat16)
    rest = (value - head.astype(jnp.float32)).astype(jnp.bfloat16)
    return head, rest


def history_kernel(
    chunks, row_hbm, col_hbm, lag_hbm, k_hbm, hist_hbm, mk_hbm, part_ref, pair_ref,
    even, odd, work, row_ref, col_ref, lag_ref, k_ref, hist_ref, mk_ref, sem, k_sem,
):
    lags, rows, points = even.shape
    entries, size = k_ref.shape[0], k_ref.shape[1]
    modes = hist_ref.shape[2]
    chunk = entries // chunks
    pairs = [(row_hbm, row_ref), (col_hbm, col_ref), (lag_hbm, lag_ref),
             (hist_hbm, hist_ref), (mk_hbm, mk_ref)]
    loads = [pltpu.make_async_copy(src, dst, sem.at[i]) for i, (src, dst) in enumerate(pairs)]

    def load_k(c):
        span = pl.ds(c * chunk, chunk)
        return pltpu.make_async_copy(k_hbm.at[span], k_ref.at[span], k_sem.at[c])

    for copy in loads[:3]:
        copy.start()
    for c in range(chunks):
        load_k(c).start()
    for copy in loads[3:]:
        copy.start()
    even[...] = jnp.zeros_like(even)
    odd[...] = jnp.zeros_like(odd)
    for copy in loads[:3]:
        copy.wait()

    def add(total, e):
        r = pl.multiple_of(row_ref[e] * size, size)
        c = pl.multiple_of(col_ref[e] * size, size)
        total[lag_ref[e], pl.ds(r, size), pl.ds(c, size)] += k_ref[e].astype(jnp.float32)

    def take(c, carry):
        load_k(c).wait()

        def body(j, carry):
            add(even, c * chunk + 2 * j)
            add(odd, c * chunk + 2 * j + 1)
            return carry

        return lax.fori_loop(0, chunk // 2, body, carry, unroll=2)

    lax.fori_loop(0, chunks, take, 0)
    for copy in loads[3:]:
        copy.wait()
    for l in range(lags):
        head, rest = split_rows(even[l] + odd[l])
        target = pair_ref.at[l] if l < BACK else work
        target[:rows, :] = head
        target[rows:, :] = rest
        count = min(l, BACK) + 1
        x = jnp.concatenate([hist_ref[l - s] for s in range(count)], axis=1)
        found = split_dot(target[...], x)
        for s in range(count):
            term = found[:, s * modes:(s + 1) * modes] * mk_ref[l:l + 1, :]
            if l == s:
                part_ref[s] = term
            else:
                part_ref[s] += term


def march_kernel(
    n, n_pts,
    part_ref, pair_ref, halo_ref, mk_ref, inc_ref, inv_ref, out_ref,
    inv_pair, field, got_c, sum_c, got_x, sum_x, got_z, sum_z,
    root_field, solved_pair, slabs, full,
    sc, rc, sw, rw, s2, r2, s3, r3, s4, r4, s5, r5, s6, r6, s7, r7, s8, s9, r9, sx, rx,
):
    me = lax.axis_index("lag")
    mine = lax.axis_index("pts")
    core = lax.rem(me, 2)
    side = lax.rem(me // 2, 2)
    z = me // 4
    groups = n // 4
    quarter = core * 2 + side
    sibling = {"lag": me + 1 - 2 * core}
    across = {"lag": me + 2 - 4 * side}
    rows = part_ref.shape[1]
    points = halo_ref.shape[1]
    size = inv_ref.shape[1]
    row_blocks = rows // size
    half = rows // 2
    wide = rows // 4
    thin = rows // n
    is_root = me == 0

    barrier = pltpu.get_barrier_semaphore()

    def loop(first, last, act):
        def body(i, carry):
            act(i)
            return carry

        lax.fori_loop(first, last, body, 0)

    def greet(k):
        pl.semaphore_signal(
            barrier, inc=1, device_id={"lag": lax.rem(me + k, n)}, device_id_type=MESH
        )

    loop(1, n, greet)
    for k in range(1, n_pts):
        pl.semaphore_signal(
            barrier, inc=1, device_id={"pts": lax.rem(mine + k, n_pts)}, device_id_type=MESH
        )

    def to(device, src, dst, send, recv):
        return pltpu.make_async_remote_copy(
            src_ref=src, dst_ref=dst, send_sem=send, recv_sem=recv,
            device_id=device, device_id_type=MESH,
        )

    def span(first, count):
        return pl.ds(pl.multiple_of(first * count, count), count)

    other = {"lag": lax.rem(me + 1, n)}
    share = span(quarter * groups + z, thin)

    def awaited(ref, send, recv):
        to(other, ref, ref, send, recv).wait_recv()

    def column(k):
        return lax.rem(z + k, groups)

    def copy_c(s):
        return to(sibling, field.at[s, span(1 - core, half)], got_c.at[s], sc.at[s], rc.at[s])

    def copy_x(s):
        return to(across, sum_c.at[s, span(1 - side, wide)], got_x.at[s], sw.at[s], rw.at[s])

    def copy_z(s, k):
        peer = column(k)
        return to({"lag": peer * 4 + lax.rem(me, 4)}, sum_x.at[s, span(peer, thin)],
                  got_z.at[s, k - 1], s2.at[s, k - 1], r2.at[s])

    def copy_root(s):
        return to({"lag": 0}, sum_z.at[s], root_field.at[s, share], s3.at[s], r3.at[s])

    def add_term(s, l):
        field[s] += mk_ref[pl.ds(l, 1), :] * split_dot(pair_ref[l], halo_ref[BACK + l - s])

    def reduce_c(s):
        field[s] = part_ref[s]

        @pl.when(jnp.logical_not(is_root))
        def _():
            loop(0, s, lambda l: add_term(s, l))

        copy_c(s).start()

    def reduce_x(s):
        copy_c(s).wait_recv()
        sum_c[s] = field[s, span(core, half), :] + got_c[s]
        copy_x(s).start()

    def reduce_z(s):
        copy_x(s).wait_recv()
        sum_x[s] = sum_c[s, span(side, wide), :] + got_x[s]
        for k in range(1, groups):
            copy_z(s, k).start()

    def reduce_root(s):
        awaited(got_z.at[s], s2.at[s, 0], r2.at[s])
        total = sum_x[s, span(z, thin), :]
        for k in range(groups - 1):
            total += got_z[s, k]

        @pl.when(is_root)
        def _():
            root_field[s, 0:thin, :] = total

        @pl.when(jnp.logical_not(is_root))
        def _():
            sum_z[s] = total
            copy_root(s).start()

    def solve(head, rest, r):
        both = jnp.dot(inv_pair[r], head, preferred_element_type=jnp.float32)
        last = jnp.dot(inv_pair[r, :size, :], rest, preferred_element_type=jnp.float32)
        return both[:size] + both[size:] + last

    def solve_pair(l):
        for r in range(row_blocks):
            block = slice(r * size, (r + 1) * size)
            below = slice(rows + r * size, rows + (r + 1) * size)
            head, rest = split_rows(solve(pair_ref[l, block, :], pair_ref[l, below, :], r))
            solved_pair[l, block, :] = head
            solved_pair[l, below, :] = rest

    def copy_pts(s, k):
        here = slabs.at[s, span(mine, rows)]
        return to({"pts": lax.rem(mine + k, n_pts)}, here, here, sx.at[s, k - 1], rx.at[s])

    def copy4(s, j):
        owner = lax.rem(j, 2) * 2 + lax.rem(j // 2, 2)
        part = full.at[s, span(owner * groups + j // 4, thin)]
        return to({"lag": j}, part, part, s4.at[s], r4.at[s])

    def copy5(s, k):
        here = full.at[s, share]
        return to({"lag": column(k) * 4 + lax.rem(me, 4)}, here, here, s5.at[s, k - 1], r5.at[s])

    def copy6(s):
        here = full.at[s, span(quarter, wide)]
        return to(across, here, here, s6.at[s], r6.at[s])

    def copy7(s):
        return to({"lag": 1}, full.at[s], full.at[s], s7.at[s], r7.at[s])

    def copy8(s, k):
        here = full.at[s, pl.ds(0, thin)]
        return to({"lag": k * 4}, here, here, s8.at[s, k - 1], r5.at[s])

    def copy8_x(s):
        here = full.at[s, pl.ds(0, wide)]
        return to({"lag": 2}, here, here, s8.at[s, groups - 1], r6.at[s])

    def copy9(s):
        here = full.at[s, span(core, half)]
        return to(sibling, here, here, s9.at[s], r9.at[s])

    def take_away(s, l):
        @pl.when(l == 0)
        def _():
            awaited(slabs.at[s - 1, pl.ds(0, points - rows)], sx.at[s - 1, 0], rx.at[s - 1])

        full[s] -= mk_ref[pl.ds(l, 1), :] * split_dot(solved_pair[l], slabs[s - 1 - l])

    def march(s):
        awaited(root_field.at[s, pl.ds(thin, rows - thin)], s3.at[s], r3.at[s])
        for r in range(row_blocks):
            block = slice(r * size, (r + 1) * size)
            net = inc_ref[s, block, :].astype(jnp.float32) - root_field[s, block, :]
            full[s, block, :] = solve(*split_rows(net), r)
        loop(0, s, lambda i: take_away(s, s - 1 - i))

        @pl.when(s < BACK)
        def _():
            slabs[s, span(mine, rows), :] = full[s].astype(jnp.bfloat16)
            for k in range(1, n_pts):
                copy_pts(s, k).start()
            copy7(s).start()
            solve_pair(s)

    def hub_of(s):
        return jnp.where(s < BACK, 1, 0)

    def needs(s, peer):
        return jnp.logical_and(peer != 0, peer != hub_of(s))

    def hand_out(s):
        hub = hub_of(s)

        @pl.when(s < BACK)
        def _():
            copy7(s).wait_recv()
            for k in range(1, groups):
                copy8(s, k).start()
            copy8_x(s).start()

        loop(hub + 1, n, lambda j: copy4(s, n + hub - j).start())
        for k in range(1, groups):
            copy5(s, k).start()
        copy6(s).start()

        @pl.when(s == BACK)
        def _():
            copy9(s).start()

    def relays(s):
        return jnp.logical_and(jnp.logical_not(is_root), me != hub_of(s))

    def pass_on(s):
        pl.when(me == hub_of(s))(lambda: hand_out(s))

        @pl.when(relays(s))
        def _():
            awaited(full.at[s, share], s4.at[s], r4.at[s])
            for k in range(1, groups):
                pl.when(needs(s, column(k) * 4 + lax.rem(me, 4)))(
                    lambda copy=copy5(s, k): copy.start())

    def fill_x(s):
        @pl.when(relays(s))
        def _():
            awaited(full.at[s, pl.ds(0, (groups - 1) * thin)], s5.at[s, 0], r5.at[s])
            pl.when(needs(s, across["lag"]))(lambda: copy6(s).start())

    def fill_c(s):
        @pl.when(relays(s))
        def _():
            copy6(s).wait_recv()
            pl.when(needs(s, sibling["lag"]))(lambda: copy9(s).start())

    def finish(s):
        pl.when(relays(s))(lambda: copy9(s).wait_recv())

    @pl.when(is_root)
    def _():
        for r in range(row_blocks):
            head, rest = split_rows(inv_ref[r * size:(r + 1) * size, :])
            inv_pair[r, :size, :] = head
            inv_pair[r, size:, :] = rest

    pl.semaphore_wait(barrier, n + n_pts - 2)

    def within(s, act):
        pl.when(jnp.logical_and(s >= 0, s < STEPS))(lambda: act(s))

    def reduce_wave(t):
        within(t, reduce_c)
        within(t - 1, reduce_x)
        within(t - 2, reduce_z)
        within(t - 3, reduce_root)
        pl.when(jnp.logical_and(is_root, t >= 3))(lambda: march(t - 3))

    loop(0, STEPS + 3, reduce_wave)

    def spread_wave(t):
        within(t, pass_on)
        within(t - 1, fill_x)
        within(t - 2, fill_c)

    loop(0, STEPS + 2, spread_wave)
    loop(0, STEPS, finish)

    out_ref[...] = full[...]

    def drain(s):
        copy_c(s).wait_send()
        copy_x(s).wait_send()
        for k in range(1, groups):
            copy_z(s, k).wait_send()
        hub = hub_of(s)

        @pl.when(jnp.logical_and(is_root, s < BACK))
        def _():
            for k in range(1, n_pts):
                copy_pts(s, k).wait_send()
            copy7(s).wait_send()

        pl.when(jnp.logical_not(is_root))(lambda: copy_root(s).wait_send())

        @pl.when(me == hub)
        def _():
            loop(hub + 1, n, lambda j: copy4(s, j).wait_send())

        @pl.when(jnp.logical_and(me == hub, s < BACK))
        def _():
            for k in range(1, groups):
                copy8(s, k).wait_send()
            copy8_x(s).wait_send()

        gives = jnp.logical_or(me == hub, jnp.logical_not(is_root))

        def sent(peer):
            return jnp.logical_and(gives, jnp.logical_or(me == hub, needs(s, peer)))

        for k in range(1, groups):
            pl.when(sent(column(k) * 4 + lax.rem(me, 4)))(
                lambda copy=copy5(s, k): copy.wait_send())
        pl.when(sent(across["lag"]))(lambda: copy6(s).wait_send())
        to_sibling = jnp.where(s < BACK, me > 1, jnp.logical_or(is_root, sibling["lag"] != 0))
        pl.when(to_sibling)(lambda: copy9(s).wait_send())

    loop(0, STEPS, drain)


def per_device(
    n, n_pts, history, incident, kernel_blocks, block_row, block_col, lag_offset, mode_kernel,
    self_inverse,
):
    lags, points, modes = history.shape
    entries, size = kernel_blocks.shape[0], kernel_blocks.shape[1]
    rows = self_inverse.shape[0]
    f32, bf16 = jnp.float32, jnp.bfloat16
    vmem = pl.BlockSpec(memory_space=pltpu.VMEM)
    hbm = pl.BlockSpec(memory_space=pltpu.HBM)
    chunks = 8
    dma = pltpu.SemaphoreType.DMA

    halo = lax.ppermute(history[lags - BACK:], "lag", [(i, i + 1) for i in range(n - 1)])

    part, pair = pl.pallas_call(
        functools.partial(history_kernel, chunks),
        out_shape=(
            jax.ShapeDtypeStruct((STEPS, rows, modes), f32),
            jax.ShapeDtypeStruct((BACK, 2 * rows, points), bf16),
        ),
        in_specs=[hbm] * 6,
        out_specs=(vmem, vmem),
        scratch_shapes=[
            pltpu.VMEM((lags, rows, points), f32),
            pltpu.VMEM((lags, rows, points), f32),
            pltpu.VMEM((2 * rows, points), bf16),
            pltpu.SMEM((entries,), jnp.int32),
            pltpu.SMEM((entries,), jnp.int32),
            pltpu.SMEM((entries,), jnp.int32),
            pltpu.VMEM((entries, size, size), bf16),
            pltpu.VMEM((lags, points, modes), bf16),
            pltpu.VMEM((lags, modes), f32),
            dma((5,)), dma((chunks,)),
        ],
        compiler_params=pltpu.CompilerParams(vmem_limit_bytes=HISTORY_BYTES),
    )(block_row, block_col, lag_offset, kernel_blocks, history, mode_kernel)

    groups = n // 4
    wide, thin = rows // 4, rows // n
    march_bytes = 8 * 1024 * 1024 + 40 * BACK * rows * points
    tops, sides = max(groups - 1, 1), max(n_pts - 1, 1)
    return pl.pallas_call(
        functools.partial(march_kernel, n, n_pts),
        out_shape=jax.ShapeDtypeStruct((STEPS, rows, modes), f32),
        in_specs=[vmem] * 6,
        out_specs=vmem,
        scratch_shapes=[
            pltpu.VMEM((rows // size, 2 * size, size), bf16),
            pltpu.VMEM((STEPS, rows, modes), f32),
            pltpu.VMEM((STEPS, rows // 2, modes), f32),
            pltpu.VMEM((STEPS, rows // 2, modes), f32),
            pltpu.VMEM((STEPS, wide, modes), f32),
            pltpu.VMEM((STEPS, wide, modes), f32),
            pltpu.VMEM((STEPS, tops, thin, modes), f32),
            pltpu.VMEM((STEPS, thin, modes), f32),
            pltpu.VMEM((STEPS, rows, modes), f32),
            pltpu.VMEM((BACK, 2 * rows, points), bf16),
            pltpu.VMEM((BACK, points, modes), bf16),
            pltpu.VMEM((STEPS, rows, modes), f32),
            dma((STEPS,)), dma((STEPS,)), dma((STEPS,)), dma((STEPS,)),
            dma((STEPS, tops)), dma((STEPS,)), dma((STEPS,)), dma((STEPS,)),
            dma((STEPS,)), dma((STEPS,)), dma((STEPS, tops)), dma((STEPS,)),
            dma((STEPS,)), dma((STEPS,)), dma((STEPS,)), dma((STEPS,)),
            dma((STEPS, tops + 1)), dma((STEPS,)), dma((STEPS,)),
            dma((BACK, sides)), dma((BACK,)),
        ],
        compiler_params=pltpu.CompilerParams(
            collective_id=0, has_side_effects=True, vmem_limit_bytes=march_bytes),
    )(part, pair, halo, mode_kernel, incident, self_inverse)


def solution(mesh):
    return jax.shard_map(
        functools.partial(per_device, mesh.shape["lag"], mesh.shape["pts"]),
        mesh=mesh,
        in_specs=(
            P("lag", None, None),
            P(None, "pts", None),
            P(("lag", "pts"), None, None),
            P(("lag", "pts")),
            P(("lag", "pts")),
            P(("lag", "pts")),
            P("lag", None),
            P("pts", None),
        ),
        out_specs=P(None, "pts", None),
        check_vma=False,
    )
```

```python
import functools
import jax
import jax.numpy as jnp
from jax import lax
from jax.experimental import pallas as pl
from jax.experimental.pallas import tpu as pltpu
from jax.sharding import PartitionSpec as P

STEPS = 4
BACK = STEPS - 1
HISTORY_BYTES = 54 * 1024 * 1024
MESH = pl.DeviceIdType.MESH


def split_dot(pair, x):
    both = jnp.dot(pair, x, preferred_element_type=jnp.float32)
    half = both.shape[0] // 2
    return both[:half] + both[half:]


def split_rows(value):
    head = value.astype(jnp.bfloat16)
    rest = (value - head.astype(jnp.float32)).astype(jnp.bfloat16)
    return head, rest


def history_kernel(
    chunks, row_hbm, col_hbm, lag_hbm, k_hbm, hist_hbm, mk_hbm, part_ref, pair_ref,
    even, odd, work, row_ref, col_ref, lag_ref, k_ref, hist_ref, mk_ref, sem, k_sem,
):
    lags, rows, points = even.shape
    entries, size = k_ref.shape[0], k_ref.shape[1]
    modes = hist_ref.shape[2]
    chunk = entries // chunks
    pairs = [(row_hbm, row_ref), (col_hbm, col_ref), (lag_hbm, lag_ref),
             (hist_hbm, hist_ref), (mk_hbm, mk_ref)]
    loads = [pltpu.make_async_copy(src, dst, sem.at[i]) for i, (src, dst) in enumerate(pairs)]

    def load_k(c):
        span = pl.ds(c * chunk, chunk)
        return pltpu.make_async_copy(k_hbm.at[span], k_ref.at[span], k_sem.at[c])

    for copy in loads[:3]:
        copy.start()
    for c in range(chunks):
        load_k(c).start()
    for copy in loads[3:]:
        copy.start()
    even[...] = jnp.zeros_like(even)
    odd[...] = jnp.zeros_like(odd)
    for copy in loads[:3]:
        copy.wait()

    def add(total, e):
        r = pl.multiple_of(row_ref[e] * size, size)
        c = pl.multiple_of(col_ref[e] * size, size)
        total[lag_ref[e], pl.ds(r, size), pl.ds(c, size)] += k_ref[e].astype(jnp.float32)

    def take(c, carry):
        load_k(c).wait()

        def body(j, carry):
            add(even, c * chunk + 2 * j)
            add(odd, c * chunk + 2 * j + 1)
            return carry

        return lax.fori_loop(0, chunk // 2, body, carry, unroll=2)

    lax.fori_loop(0, chunks, take, 0)
    for copy in loads[3:]:
        copy.wait()
    for l in range(lags):
        head, rest = split_rows(even[l] + odd[l])
        target = pair_ref.at[l] if l < BACK else work
        target[:rows, :] = head
        target[rows:, :] = rest
        count = min(l, BACK) + 1
        x = jnp.concatenate([hist_ref[l - s] for s in range(count)], axis=1)
        found = split_dot(target[...], x)
        for s in range(count):
            term = found[:, s * modes:(s + 1) * modes] * mk_ref[l:l + 1, :]
            if l == s:
                part_ref[s] = term
            else:
                part_ref[s] += term


def march_kernel(
    n, n_pts,
    part_ref, pair_ref, halo_ref, mk_ref, inc_ref, inv_ref, out_ref,
    inv_pair, field, got, share_sum, root_field, solved_pair, slabs, full,
    sa, ra, s3, r3, s4, r4, s5, r5, s6, r6, s7, r7, s8, sx, rx,
):
    me = lax.axis_index("lag")
    mine = lax.axis_index("pts")
    z = me // 4
    groups = n // 4
    quarter = lax.rem(me, 4)
    rows = part_ref.shape[1]
    points = halo_ref.shape[1]
    size = inv_ref.shape[1]
    row_blocks = rows // size
    wide = rows // 4
    thin = rows // n
    is_root = me == 0

    barrier = pltpu.get_barrier_semaphore()

    def loop(first, last, act):
        def body(i, carry):
            act(i)
            return carry

        lax.fori_loop(first, last, body, 0)

    def greet(k):
        pl.semaphore_signal(
            barrier, inc=1, device_id={"lag": lax.rem(me + k, n)}, device_id_type=MESH
        )

    loop(1, n, greet)
    for k in range(1, n_pts):
        pl.semaphore_signal(
            barrier, inc=1, device_id={"pts": lax.rem(mine + k, n_pts)}, device_id_type=MESH
        )

    def to(device, src, dst, send, recv):
        return pltpu.make_async_remote_copy(
            src_ref=src, dst_ref=dst, send_sem=send, recv_sem=recv,
            device_id=device, device_id_type=MESH,
        )

    def span(first, count):
        return pl.ds(pl.multiple_of(first * count, count), count)

    other = {"lag": lax.rem(me + 1, n)}

    def share_of(j):
        return span(lax.rem(j, 4) * groups + j // 4, thin)

    share = share_of(me)

    def awaited(ref, send, recv):
        to(other, ref, ref, send, recv).wait_recv()

    def column(k):
        return lax.rem(z + k, groups)

    def in_group(k):
        return z * 4 + lax.rem(me + k, 4)

    def copy_a(s, k):
        peer = lax.rem(me + k, n)
        return to({"lag": peer}, field.at[s, share_of(peer)], got.at[s, k - 1], sa.at[s], ra.at[s])

    def copy_root(s):
        return to({"lag": 0}, share_sum.at[s], root_field.at[s, share], s3.at[s], r3.at[s])

    def add_term(s, l):
        field[s] += mk_ref[pl.ds(l, 1), :] * split_dot(pair_ref[l], halo_ref[BACK + l - s])

    def reduce_all(s):
        field[s] = part_ref[s]

        @pl.when(jnp.logical_not(is_root))
        def _():
            loop(0, s, lambda l: add_term(s, l))

        loop(1, n, lambda k: copy_a(s, k).start())

    def reduce_root(s):
        awaited(got.at[s], sa.at[s], ra.at[s])
        total = field[s, share, :]
        for k in range(n - 1):
            total += got[s, k]

        @pl.when(is_root)
        def _():
            root_field[s, 0:thin, :] = total

        @pl.when(jnp.logical_not(is_root))
        def _():
            share_sum[s] = total
            copy_root(s).start()

    def solve(head, rest, r):
        both = jnp.dot(inv_pair[r], head, preferred_element_type=jnp.float32)
        last = jnp.dot(inv_pair[r, :size, :], rest, preferred_element_type=jnp.float32)
        return both[:size] + both[size:] + last

    def solve_pair(l):
        for r in range(row_blocks):
            block = slice(r * size, (r + 1) * size)
            below = slice(rows + r * size, rows + (r + 1) * size)
            head, rest = split_rows(solve(pair_ref[l, block, :], pair_ref[l, below, :], r))
            solved_pair[l, block, :] = head
            solved_pair[l, below, :] = rest

    def copy_pts(s, k):
        here = slabs.at[s, span(mine, rows)]
        return to({"pts": lax.rem(mine + k, n_pts)}, here, here, sx.at[s, k - 1], rx.at[s])

    def copy4(s, j):
        part = full.at[s, share_of(j)]
        return to({"lag": j}, part, part, s4.at[s], r4.at[s])

    def copy5(s, k):
        here = full.at[s, share]
        return to({"lag": column(k) * 4 + quarter}, here, here, s5.at[s, k - 1], r5.at[s])

    def copy6(s, k):
        here = full.at[s, span(quarter, wide)]
        return to({"lag": in_group(k)}, here, here, s6.at[s, k - 1], r6.at[s])

    def copy7(s):
        return to({"lag": 1}, full.at[s], full.at[s], s7.at[s], r7.at[s])

    def copy8(s, k):
        here = full.at[s, pl.ds(0, thin)]
        return to({"lag": k * 4}, here, here, s8.at[s, k - 1], r5.at[s])

    def copy8_q(s, k):
        here = full.at[s, pl.ds(0, wide)]
        return to({"lag": k}, here, here, s8.at[s, groups + k - 3], r6.at[s])

    def take_away(s, l):
        @pl.when(l == 0)
        def _():
            awaited(slabs.at[s - 1, pl.ds(0, points - rows)], sx.at[s - 1, 0], rx.at[s - 1])

        full[s] -= mk_ref[pl.ds(l, 1), :] * split_dot(solved_pair[l], slabs[s - 1 - l])

    def march(s):
        awaited(root_field.at[s, pl.ds(thin, rows - thin)], s3.at[s], r3.at[s])
        for r in range(row_blocks):
            block = slice(r * size, (r + 1) * size)
            net = inc_ref[s, block, :].astype(jnp.float32) - root_field[s, block, :]
            full[s, block, :] = solve(*split_rows(net), r)
        loop(0, s, lambda i: take_away(s, s - 1 - i))

        @pl.when(s < BACK)
        def _():
            slabs[s, span(mine, rows), :] = full[s].astype(jnp.bfloat16)
            for k in range(1, n_pts):
                copy_pts(s, k).start()
            copy7(s).start()
            solve_pair(s)

    def hub_of(s):
        return jnp.where(s < BACK, 1, 0)

    def needs(s, peer):
        return jnp.logical_and(peer != 0, peer != hub_of(s))

    def hand_out(s):
        hub = hub_of(s)

        @pl.when(s < BACK)
        def _():
            copy7(s).wait_recv()
            for k in range(1, groups):
                copy8(s, k).start()
            for k in range(2, 4):
                copy8_q(s, k).start()

        loop(hub + 1, n, lambda j: copy4(s, n + hub - j).start())
        for k in range(1, groups):
            copy5(s, k).start()
        for k in range(1, 4):
            pl.when(jnp.logical_or(is_root, in_group(k) != 0))(
                lambda copy=copy6(s, k): copy.start())

    def relays(s):
        return jnp.logical_and(jnp.logical_not(is_root), me != hub_of(s))

    def pass_on(s):
        pl.when(me == hub_of(s))(lambda: hand_out(s))

        @pl.when(relays(s))
        def _():
            awaited(full.at[s, share], s4.at[s], r4.at[s])
            for k in range(1, groups):
                pl.when(needs(s, column(k) * 4 + quarter))(
                    lambda copy=copy5(s, k): copy.start())

    def fill_x(s):
        @pl.when(relays(s))
        def _():
            awaited(full.at[s, pl.ds(0, (groups - 1) * thin)], s5.at[s, 0], r5.at[s])
            for k in range(1, 4):
                pl.when(needs(s, in_group(k)))(lambda copy=copy6(s, k): copy.start())

    def finish(s):
        pl.when(relays(s))(
            lambda: awaited(full.at[s, pl.ds(0, 3 * wide)], s6.at[s, 0], r6.at[s]))

    @pl.when(is_root)
    def _():
        for r in range(row_blocks):
            head, rest = split_rows(inv_ref[r * size:(r + 1) * size, :])
            inv_pair[r, :size, :] = head
            inv_pair[r, size:, :] = rest

    pl.semaphore_wait(barrier, n + n_pts - 2)

    def within(s, act):
        pl.when(jnp.logical_and(s >= 0, s < STEPS))(lambda: act(s))

    def reduce_wave(t):
        within(t, reduce_all)
        within(t - 1, reduce_root)
        pl.when(jnp.logical_and(is_root, t >= 2))(lambda: march(t - 2))

    loop(0, STEPS + 2, reduce_wave)

    def spread_wave(t):
        within(t, pass_on)
        within(t - 1, fill_x)

    loop(0, STEPS + 1, spread_wave)
    loop(0, STEPS, finish)

    out_ref[...] = full[...]

    def drain(s):
        rest = field.at[s, pl.ds(0, rows - thin)]
        to(other, rest, rest, sa.at[s], ra.at[s]).wait_send()
        hub = hub_of(s)

        @pl.when(jnp.logical_and(is_root, s < BACK))
        def _():
            for k in range(1, n_pts):
                copy_pts(s, k).wait_send()
            copy7(s).wait_send()

        pl.when(jnp.logical_not(is_root))(lambda: copy_root(s).wait_send())

        @pl.when(me == hub)
        def _():
            loop(hub + 1, n, lambda j: copy4(s, j).wait_send())

        @pl.when(jnp.logical_and(me == hub, s < BACK))
        def _():
            for k in range(1, groups):
                copy8(s, k).wait_send()
            for k in range(2, 4):
                copy8_q(s, k).wait_send()

        gives = jnp.logical_or(me == hub, jnp.logical_not(is_root))

        def sent(peer):
            return jnp.logical_and(gives, jnp.logical_or(me == hub, needs(s, peer)))

        for k in range(1, groups):
            pl.when(sent(column(k) * 4 + quarter))(
                lambda copy=copy5(s, k): copy.wait_send())
        for k in range(1, 4):
            peer = in_group(k)
            reached = jnp.where(me == hub, jnp.logical_or(is_root, peer != 0), sent(peer))
            pl.when(reached)(lambda copy=copy6(s, k): copy.wait_send())

    loop(0, STEPS, drain)


def per_device(
    n, n_pts, history, incident, kernel_blocks, block_row, block_col, lag_offset, mode_kernel,
    self_inverse,
):
    lags, points, modes = history.shape
    entries, size = kernel_blocks.shape[0], kernel_blocks.shape[1]
    rows = self_inverse.shape[0]
    f32, bf16 = jnp.float32, jnp.bfloat16
    vmem = pl.BlockSpec(memory_space=pltpu.VMEM)
    hbm = pl.BlockSpec(memory_space=pltpu.HBM)
    chunks = 8
    dma = pltpu.SemaphoreType.DMA

    halo = lax.ppermute(history[lags - BACK:], "lag", [(i, i + 1) for i in range(n - 1)])

    part, pair = pl.pallas_call(
        functools.partial(history_kernel, chunks),
        out_shape=(
            jax.ShapeDtypeStruct((STEPS, rows, modes), f32),
            jax.ShapeDtypeStruct((BACK, 2 * rows, points), bf16),
        ),
        in_specs=[hbm] * 6,
        out_specs=(vmem, vmem),
        scratch_shapes=[
            pltpu.VMEM((lags, rows, points), f32),
            pltpu.VMEM((lags, rows, points), f32),
            pltpu.VMEM((2 * rows, points), bf16),
            pltpu.SMEM((entries,), jnp.int32),
            pltpu.SMEM((entries,), jnp.int32),
            pltpu.SMEM((entries,), jnp.int32),
            pltpu.VMEM((entries, size, size), bf16),
            pltpu.VMEM((lags, points, modes), bf16),
            pltpu.VMEM((lags, modes), f32),
            dma((5,)), dma((chunks,)),
        ],
        compiler_params=pltpu.CompilerParams(vmem_limit_bytes=HISTORY_BYTES),
    )(block_row, block_col, lag_offset, kernel_blocks, history, mode_kernel)

    groups = n // 4
    thin = rows // n
    march_bytes = 8 * 1024 * 1024 + 40 * BACK * rows * points
    tops, sides = max(groups - 1, 1), max(n_pts - 1, 1)
    return pl.pallas_call(
        functools.partial(march_kernel, n, n_pts),
        out_shape=jax.ShapeDtypeStruct((STEPS, rows, modes), f32),
        in_specs=[vmem] * 6,
        out_specs=vmem,
        scratch_shapes=[
            pltpu.VMEM((rows // size, 2 * size, size), bf16),
            pltpu.VMEM((STEPS, rows, modes), f32),
            pltpu.VMEM((STEPS, n - 1, thin, modes), f32),
            pltpu.VMEM((STEPS, thin, modes), f32),
            pltpu.VMEM((STEPS, rows, modes), f32),
            pltpu.VMEM((BACK, 2 * rows, points), bf16),
            pltpu.VMEM((BACK, points, modes), bf16),
            pltpu.VMEM((STEPS, rows, modes), f32),
            dma((STEPS,)), dma((STEPS,)), dma((STEPS,)), dma((STEPS,)),
            dma((STEPS,)), dma((STEPS,)), dma((STEPS, tops)), dma((STEPS,)),
            dma((STEPS, 3)), dma((STEPS,)), dma((STEPS,)), dma((STEPS,)),
            dma((STEPS, tops + 2)),
            dma((BACK, sides)), dma((BACK,)),
        ],
        compiler_params=pltpu.CompilerParams(
            collective_id=0, has_side_effects=True, vmem_limit_bytes=march_bytes),
    )(part, pair, halo, mode_kernel, incident, self_inverse)


def solution(mesh):
    return jax.shard_map(
        functools.partial(per_device, mesh.shape["lag"], mesh.shape["pts"]),
        mesh=mesh,
        in_specs=(
            P("lag", None, None),
            P(None, "pts", None),
            P(("lag", "pts"), None, None),
            P(("lag", "pts")),
            P(("lag", "pts")),
            P(("lag", "pts")),
            P("lag", None),
            P("pts", None),
        ),
        out_specs=P(None, "pts", None),
        check_vma=False,
    )
```

```python
import functools
import jax
import jax.numpy as jnp
from jax import lax
from jax.experimental import pallas as pl
from jax.experimental.pallas import tpu as pltpu
from jax.sharding import PartitionSpec as P

STEPS = 4
BACK = STEPS - 1
HISTORY_BYTES = 54 * 1024 * 1024
MESH = pl.DeviceIdType.MESH


def split_dot(pair, x):
    both = jnp.dot(pair, x, preferred_element_type=jnp.float32)
    half = both.shape[0] // 2
    return both[:half] + both[half:]


def split_rows(value):
    head = value.astype(jnp.bfloat16)
    rest = (value - head.astype(jnp.float32)).astype(jnp.bfloat16)
    return head, rest


def history_kernel(
    chunks, row_hbm, col_hbm, lag_hbm, k_hbm, hist_hbm, mk_hbm, part_ref, pair_ref,
    even, odd, work, row_ref, col_ref, lag_ref, k_ref, hist_ref, mk_ref, sem, k_sem,
):
    lags, rows, points = even.shape
    entries, size = k_ref.shape[0], k_ref.shape[1]
    modes = hist_ref.shape[2]
    chunk = entries // chunks
    pairs = [(row_hbm, row_ref), (col_hbm, col_ref), (lag_hbm, lag_ref),
             (hist_hbm, hist_ref), (mk_hbm, mk_ref)]
    loads = [pltpu.make_async_copy(src, dst, sem.at[i]) for i, (src, dst) in enumerate(pairs)]

    def load_k(c):
        span = pl.ds(c * chunk, chunk)
        return pltpu.make_async_copy(k_hbm.at[span], k_ref.at[span], k_sem.at[c])

    for copy in loads[:3]:
        copy.start()
    for c in range(chunks):
        load_k(c).start()
    for copy in loads[3:]:
        copy.start()
    even[...] = jnp.zeros_like(even)
    odd[...] = jnp.zeros_like(odd)
    for copy in loads[:3]:
        copy.wait()

    def add(total, e):
        r = pl.multiple_of(row_ref[e] * size, size)
        c = pl.multiple_of(col_ref[e] * size, size)
        total[lag_ref[e], pl.ds(r, size), pl.ds(c, size)] += k_ref[e].astype(jnp.float32)

    def take(c, carry):
        load_k(c).wait()

        def body(j, carry):
            add(even, c * chunk + 2 * j)
            add(odd, c * chunk + 2 * j + 1)
            return carry

        return lax.fori_loop(0, chunk // 2, body, carry, unroll=2)

    lax.fori_loop(0, chunks, take, 0)
    for copy in loads[3:]:
        copy.wait()
    for l in range(lags):
        head, rest = split_rows(even[l] + odd[l])
        target = pair_ref.at[l] if l < BACK else work
        target[:rows, :] = head
        target[rows:, :] = rest
        count = min(l, BACK) + 1
        x = jnp.concatenate([hist_ref[l - s] for s in range(count)], axis=1)
        found = split_dot(target[...], x)
        for s in range(count):
            term = found[:, s * modes:(s + 1) * modes] * mk_ref[l:l + 1, :]
            if l == s:
                part_ref[s] = term
            else:
                part_ref[s] += term


def march_kernel(
    n, n_pts,
    part_ref, pair_ref, halo_ref, mk_ref, inc_ref, inv_ref, out_ref,
    inv_pair, field, got, share_sum, root_field, solved_pair, slabs, full,
    sa, ra, s3, r3, s4, r4, s5, r5, s6, r6, s7, r7, s8, sx, rx,
):
    me = lax.axis_index("lag")
    mine = lax.axis_index("pts")
    z = me // 4
    groups = n // 4
    quarter = lax.rem(me, 4)
    rows = part_ref.shape[1]
    points = halo_ref.shape[1]
    size = inv_ref.shape[1]
    row_blocks = rows // size
    wide = rows // 4
    thin = rows // n
    is_root = me == 0

    barrier = pltpu.get_barrier_semaphore()

    def loop(first, last, act):
        def body(i, carry):
            act(i)
            return carry

        lax.fori_loop(first, last, body, 0)

    def greet(k):
        pl.semaphore_signal(
            barrier, inc=1, device_id={"lag": lax.rem(me + k, n)}, device_id_type=MESH
        )

    loop(1, n, greet)
    for k in range(1, n_pts):
        pl.semaphore_signal(
            barrier, inc=1, device_id={"pts": lax.rem(mine + k, n_pts)}, device_id_type=MESH
        )

    def to(device, src, dst, send, recv):
        return pltpu.make_async_remote_copy(
            src_ref=src, dst_ref=dst, send_sem=send, recv_sem=recv,
            device_id=device, device_id_type=MESH,
        )

    def span(first, count):
        return pl.ds(pl.multiple_of(first * count, count), count)

    other = {"lag": lax.rem(me + 1, n)}

    def share_of(j):
        return span(lax.rem(j, 4) * groups + j // 4, thin)

    share = share_of(me)

    def awaited(ref, send, recv):
        to(other, ref, ref, send, recv).wait_recv()

    def column(k):
        return lax.rem(z + k, groups)

    def in_group(k):
        return z * 4 + lax.rem(me + k, 4)

    def copy_a(s, k):
        peer = lax.rem(me + k, n)
        return to({"lag": peer}, field.at[s, share_of(peer)], got.at[s, k - 1], sa.at[s], ra.at[s])

    def copy_root(s):
        return to({"lag": 0}, share_sum.at[s], root_field.at[s, share], s3.at[s], r3.at[s])

    def add_term(s, l):
        field[s] += mk_ref[pl.ds(l, 1), :] * split_dot(pair_ref[l], halo_ref[BACK + l - s])

    def reduce_all(s):
        field[s] = part_ref[s]

        @pl.when(jnp.logical_not(is_root))
        def _():
            loop(0, s, lambda l: add_term(s, l))

        loop(1, n, lambda k: copy_a(s, k).start())

    def reduce_root(s):
        awaited(got.at[s], sa.at[s], ra.at[s])
        total = field[s, share, :]
        for k in range(n - 1):
            total += got[s, k]

        @pl.when(is_root)
        def _():
            root_field[s, 0:thin, :] = total

        @pl.when(jnp.logical_not(is_root))
        def _():
            share_sum[s] = total
            copy_root(s).start()

    def solve(head, rest, r):
        both = jnp.dot(inv_pair[r], head, preferred_element_type=jnp.float32)
        last = jnp.dot(inv_pair[r, :size, :], rest, preferred_element_type=jnp.float32)
        return both[:size] + both[size:] + last

    def solve_pair(l):
        for r in range(row_blocks):
            block = slice(r * size, (r + 1) * size)
            below = slice(rows + r * size, rows + (r + 1) * size)
            head, rest = split_rows(solve(pair_ref[l, block, :], pair_ref[l, below, :], r))
            solved_pair[l, block, :] = head
            solved_pair[l, below, :] = rest

    def copy_pts(s, k):
        here = slabs.at[s, span(mine, rows)]
        return to({"pts": lax.rem(mine + k, n_pts)}, here, here, sx.at[s, k - 1], rx.at[s])

    def copy4(s, j):
        part = full.at[s, share_of(j)]
        return to({"lag": j}, part, part, s4.at[s], r4.at[s])

    def copy5(s, k):
        here = full.at[s, share]
        return to({"lag": column(k) * 4 + quarter}, here, here, s5.at[s, k - 1], r5.at[s])

    def copy6(s, k):
        here = full.at[s, span(quarter, wide)]
        return to({"lag": in_group(k)}, here, here, s6.at[s, k - 1], r6.at[s])

    def copy7(s):
        return to({"lag": 1}, full.at[s], full.at[s], s7.at[s], r7.at[s])

    def copy8(s, k):
        here = full.at[s, pl.ds(0, thin)]
        return to({"lag": k * 4}, here, here, s8.at[s, k - 1], r5.at[s])

    def copy8_q(s, k):
        here = full.at[s, pl.ds(0, wide)]
        return to({"lag": k}, here, here, s8.at[s, groups + k - 3], r6.at[s])

    def take_away(s, l):
        @pl.when(l == 0)
        def _():
            awaited(slabs.at[s - 1, pl.ds(0, points - rows)], sx.at[s - 1, 0], rx.at[s - 1])

        full[s] -= mk_ref[pl.ds(l, 1), :] * split_dot(solved_pair[l], slabs[s - 1 - l])

    def march(s):
        awaited(root_field.at[s, pl.ds(thin, rows - thin)], s3.at[s], r3.at[s])
        for r in range(row_blocks):
            block = slice(r * size, (r + 1) * size)
            net = inc_ref[s, block, :].astype(jnp.float32) - root_field[s, block, :]
            full[s, block, :] = solve(*split_rows(net), r)
        loop(0, s, lambda i: take_away(s, s - 1 - i))

        @pl.when(s < BACK)
        def _():
            slabs[s, span(mine, rows), :] = full[s].astype(jnp.bfloat16)
            for k in range(1, n_pts):
                copy_pts(s, k).start()
            copy7(s).start()

    def hub_of(s):
        return jnp.where(s < BACK, 1, 0)

    def needs(s, peer):
        return jnp.logical_and(peer != 0, peer != hub_of(s))

    def hand_out(s):
        hub = hub_of(s)

        @pl.when(s < BACK)
        def _():
            copy7(s).wait_recv()
            for k in range(1, groups):
                copy8(s, k).start()
            for k in range(2, 4):
                copy8_q(s, k).start()

        loop(hub + 1, n, lambda j: copy4(s, n + hub - j).start())
        for k in range(1, groups):
            copy5(s, k).start()
        for k in range(1, 4):
            pl.when(jnp.logical_or(is_root, in_group(k) != 0))(
                lambda copy=copy6(s, k): copy.start())

    def relays(s):
        return jnp.logical_and(jnp.logical_not(is_root), me != hub_of(s))

    def pass_on(s):
        pl.when(me == hub_of(s))(lambda: hand_out(s))

        @pl.when(relays(s))
        def _():
            awaited(full.at[s, share], s4.at[s], r4.at[s])
            for k in range(1, groups):
                pl.when(needs(s, column(k) * 4 + quarter))(
                    lambda copy=copy5(s, k): copy.start())

    def fill_x(s):
        @pl.when(relays(s))
        def _():
            awaited(full.at[s, pl.ds(0, (groups - 1) * thin)], s5.at[s, 0], r5.at[s])
            for k in range(1, 4):
                pl.when(needs(s, in_group(k)))(lambda copy=copy6(s, k): copy.start())

    def finish(s):
        pl.when(relays(s))(
            lambda: awaited(full.at[s, pl.ds(0, 3 * wide)], s6.at[s, 0], r6.at[s]))

    @pl.when(is_root)
    def _():
        for r in range(row_blocks):
            head, rest = split_rows(inv_ref[r * size:(r + 1) * size, :])
            inv_pair[r, :size, :] = head
            inv_pair[r, size:, :] = rest

    pl.semaphore_wait(barrier, n + n_pts - 2)

    def within(s, act):
        pl.when(jnp.logical_and(s >= 0, s < STEPS))(lambda: act(s))

    def reduce_wave(t):
        pl.when(jnp.logical_and(jnp.logical_not(is_root), t < STEPS))(lambda: reduce_all(t))
        within(t - 1, reduce_root)
        pl.when(jnp.logical_and(is_root, t >= 2))(lambda: march(t - 2))

    @pl.when(is_root)
    def _():
        loop(0, STEPS, reduce_all)
        loop(0, BACK, solve_pair)

    loop(0, STEPS + 2, reduce_wave)

    def spread_wave(t):
        within(t, pass_on)
        within(t - 1, fill_x)

    loop(0, STEPS + 1, spread_wave)
    loop(0, STEPS, finish)

    out_ref[...] = full[...]

    def drain(s):
        rest = field.at[s, pl.ds(0, rows - thin)]
        to(other, rest, rest, sa.at[s], ra.at[s]).wait_send()
        hub = hub_of(s)

        @pl.when(jnp.logical_and(is_root, s < BACK))
        def _():
            for k in range(1, n_pts):
                copy_pts(s, k).wait_send()
            copy7(s).wait_send()

        pl.when(jnp.logical_not(is_root))(lambda: copy_root(s).wait_send())

        @pl.when(me == hub)
        def _():
            loop(hub + 1, n, lambda j: copy4(s, j).wait_send())

        @pl.when(jnp.logical_and(me == hub, s < BACK))
        def _():
            for k in range(1, groups):
                copy8(s, k).wait_send()
            for k in range(2, 4):
                copy8_q(s, k).wait_send()

        gives = jnp.logical_or(me == hub, jnp.logical_not(is_root))

        def sent(peer):
            return jnp.logical_and(gives, jnp.logical_or(me == hub, needs(s, peer)))

        for k in range(1, groups):
            pl.when(sent(column(k) * 4 + quarter))(
                lambda copy=copy5(s, k): copy.wait_send())
        for k in range(1, 4):
            peer = in_group(k)
            reached = jnp.where(me == hub, jnp.logical_or(is_root, peer != 0), sent(peer))
            pl.when(reached)(lambda copy=copy6(s, k): copy.wait_send())

    loop(0, STEPS, drain)


def per_device(
    n, n_pts, history, incident, kernel_blocks, block_row, block_col, lag_offset, mode_kernel,
    self_inverse,
):
    lags, points, modes = history.shape
    entries, size = kernel_blocks.shape[0], kernel_blocks.shape[1]
    rows = self_inverse.shape[0]
    f32, bf16 = jnp.float32, jnp.bfloat16
    vmem = pl.BlockSpec(memory_space=pltpu.VMEM)
    hbm = pl.BlockSpec(memory_space=pltpu.HBM)
    chunks = 8
    dma = pltpu.SemaphoreType.DMA

    halo = lax.ppermute(history[lags - BACK:], "lag", [(i, i + 1) for i in range(n - 1)])

    part, pair = pl.pallas_call(
        functools.partial(history_kernel, chunks),
        out_shape=(
            jax.ShapeDtypeStruct((STEPS, rows, modes), f32),
            jax.ShapeDtypeStruct((BACK, 2 * rows, points), bf16),
        ),
        in_specs=[hbm] * 6,
        out_specs=(vmem, vmem),
        scratch_shapes=[
            pltpu.VMEM((lags, rows, points), f32),
            pltpu.VMEM((lags, rows, points), f32),
            pltpu.VMEM((2 * rows, points), bf16),
            pltpu.SMEM((entries,), jnp.int32),
            pltpu.SMEM((entries,), jnp.int32),
            pltpu.SMEM((entries,), jnp.int32),
            pltpu.VMEM((entries, size, size), bf16),
            pltpu.VMEM((lags, points, modes), bf16),
            pltpu.VMEM((lags, modes), f32),
            dma((5,)), dma((chunks,)),
        ],
        compiler_params=pltpu.CompilerParams(vmem_limit_bytes=HISTORY_BYTES),
    )(block_row, block_col, lag_offset, kernel_blocks, history, mode_kernel)

    groups = n // 4
    thin = rows // n
    march_bytes = 8 * 1024 * 1024 + 40 * BACK * rows * points
    tops, sides = max(groups - 1, 1), max(n_pts - 1, 1)
    return pl.pallas_call(
        functools.partial(march_kernel, n, n_pts),
        out_shape=jax.ShapeDtypeStruct((STEPS, rows, modes), f32),
        in_specs=[vmem] * 6,
        out_specs=vmem,
        scratch_shapes=[
            pltpu.VMEM((rows // size, 2 * size, size), bf16),
            pltpu.VMEM((STEPS, rows, modes), f32),
            pltpu.VMEM((STEPS, n - 1, thin, modes), f32),
            pltpu.VMEM((STEPS, thin, modes), f32),
            pltpu.VMEM((STEPS, rows, modes), f32),
            pltpu.VMEM((BACK, 2 * rows, points), bf16),
            pltpu.VMEM((BACK, points, modes), bf16),
            pltpu.VMEM((STEPS, rows, modes), f32),
            dma((STEPS,)), dma((STEPS,)), dma((STEPS,)), dma((STEPS,)),
            dma((STEPS,)), dma((STEPS,)), dma((STEPS, tops)), dma((STEPS,)),
            dma((STEPS, 3)), dma((STEPS,)), dma((STEPS,)), dma((STEPS,)),
            dma((STEPS, tops + 2)),
            dma((BACK, sides)), dma((BACK,)),
        ],
        compiler_params=pltpu.CompilerParams(
            collective_id=0, has_side_effects=True, vmem_limit_bytes=march_bytes),
    )(part, pair, halo, mode_kernel, incident, self_inverse)


def solution(mesh):
    return jax.shard_map(
        functools.partial(per_device, mesh.shape["lag"], mesh.shape["pts"]),
        mesh=mesh,
        in_specs=(
            P("lag", None, None),
            P(None, "pts", None),
            P(("lag", "pts"), None, None),
            P(("lag", "pts")),
            P(("lag", "pts")),
            P(("lag", "pts")),
            P("lag", None),
            P("pts", None),
        ),
        out_specs=P(None, "pts", None),
        check_vma=False,
    )
```
